512 devices in a mesh: expert: 8 (over z_lo, core), dp: 64 (over z_hi, x, y).
Axes of the slice: x: 4, y: 4, z: 16 (z_hi: 4, z_lo: 4; z = z_hi * 4 + z_lo), core: 2. Of those that a mesh axis runs over, the one named last changes fastest.
Arguments:
- out_grad: bfloat16 [4096, 3072], P(('expert', 'dp')), may hold values from -6 to 6
- gate_saved: bfloat16 [4096, 2, 8192], P('expert', None, 'dp'), may hold values from -6 to 6
- up_saved: bfloat16 [4096, 2, 8192], P('expert', None, 'dp'), may hold values from -6 to 6
- routing: int32 [4096, 2], P('expert'), may hold values from 0 to 7, all different within a row; in each aligned block of 512 rows (0 to 511, 512 to 1023, ...) at most 256 rows name the same one
- down_weight: bfloat16 [8, 3072, 8192], P('expert', None, 'dp'), may hold values from -0.0625 to 0.0625
- momentum: bfloat16 [8, 3072, 8192], P('expert', 'dp'), may hold values from -60 to 60
Outputs:
- d_gate: bfloat16 [4096, 2, 8192], P('expert', None, 'dp')
- d_up: bfloat16 [4096, 2, 8192], P('expert', None, 'dp')
- new_weight: float32 [8, 3072, 8192], P('expert', 'dp')
- new_momentum: bfloat16 [8, 3072, 8192], P('expert', 'dp')
The draws below stay inside these ranges and needn't reach their ends.
Inputs may be any that keep to these rules, and one draw needn't show every extreme that they name: `routing`: in each aligned block of 512 tokens (one group), the 2 experts of a token differ, no expert is named by more than 256 tokens, a bound that some block reaches.
All inputs are finite; a program needn't handle non-finite values.
Results may differ from the reference program's by a relative error of at most 0.0015.
Values may be sent and summed in bfloat16 or wider, within the bound.
A program may use at most 128 MiB of HBM per device.

```python
import math
import jax
import jax.numpy as jnp
import numpy as np

D = 3072
FF = 8192
TOPK = 2
GROUP_TOK = 512
EXPERTS = 8
TOKENS = 4096
CAP = 256


def level_of(rng, dims, cuts, low, high):
    def one(dim, blocks):
        steps = jax.random.uniform(jax.random.fold_in(jax.random.fold_in(rng, 6), dim), (blocks,), jnp.float32, low / len(cuts), high / len(cuts))
        return jnp.repeat(jnp.exp(steps), dims[dim] // blocks).reshape((-1,) + (1,) * (len(dims) - dim - 1))

    loudness = one(*cuts[0])
    for cut in cuts[1:]:
        loudness = loudness * one(*cut)
    return loudness


def routed_block(rng, own, number, rows, number_of, top, bound, skew):
    order = jax.random.permutation(rng, number_of)
    heavy_load, common = portions_of(number_of, rows * top, bound, skew, True), portions_of(number_of, rows * top, bound, skew, False)
    places = jnp.arange(number_of)

    def named(tallies, rotation):
        used = int((tallies > 0).sum())
        fixed = max(1, used // 4)
        passed = fixed + (places - fixed + rotation * (used - fixed)) % max(1, number_of - fixed)
        return jnp.zeros((number_of,), jnp.int32).at[order[jnp.where(places < fixed, places, passed)]].set(jnp.asarray(tallies, jnp.int32))

    tallies = jnp.where(number % 4 == 0, named(heavy_load, number // 4), named(common, number - number // 4 - 1))
    mixed = jax.random.permutation(jax.random.fold_in(own, 3), number_of)
    giver, receiver = mixed[0:number_of // 2 * 2:2], mixed[1:number_of // 2 * 2:2]
    slack = jnp.minimum(tallies[giver] - 1, bound - tallies[receiver]) // 2
    slack = jnp.where((giver == order[0]) | (receiver == order[0]) | (tallies[receiver] == 0), 0, jnp.maximum(slack, 0))
    passed = jax.random.randint(jax.random.fold_in(own, 4), (number_of // 2,), 0, 1 << 20) % (slack + 1)
    tallies = tallies.at[giver].add(-passed).at[receiver].add(passed)
    labels = jnp.searchsorted(jnp.cumsum(tallies), jnp.arange(rows * top), side="right").astype(jnp.int32)
    table = labels.reshape(top, rows).T
    table = table[jax.random.permutation(jax.random.fold_in(own, 1), rows)]
    rotation = jax.random.randint(jax.random.fold_in(own, 2), (rows, 1), 0, top)
    return jnp.take_along_axis(table, (jnp.arange(top)[None, :] + rotation) % top, axis=1)


def portions_of(count, total, most, slope, full):
    portions = [(1 << 20) // math.isqrt(standing ** slope) + 1 for standing in range(1, count + 1)]
    largest = most if full else min(most, max(-(-total // count), total * portions[0] // sum(portions)))
    least = 1 if total - largest >= count - 1 else 0
    counts, surplus = [largest] + [least] * (count - 1), total - largest - least * (count - 1)
    while surplus > 0:
        movable = [i for i in range(1, count) if counts[i] < largest] or [i for i in range(1, count) if counts[i] < most]
        mass, left = sum([portions[i] for i in movable]), surplus
        for i in movable:
            extra = min(most - counts[i], max(1, left * portions[i] // mass), surplus)
            counts[i] = counts[i] + extra
            surplus = surplus - extra
    return np.array(counts)


def centred(own_key, extent, spread, limit, pieces=(), held_as=jnp.bfloat16):
    array = jax.random.normal(own_key, extent, jnp.float32) * spread
    if len(pieces) > 0:
        array = level_of(own_key, extent, pieces, -0.22, 0.18) * array
    return jnp.clip(array, min=-limit, max=limit).astype(held_as)


def setup_inputs(seed: int = 0) -> dict:
    splits = jax.random.split(jax.random.key(seed), 7)
    out_grad = centred(splits[0], (TOKENS, D), 1.0, 6.0, ((0, 512),))
    gate_saved = centred(splits[1], (TOKENS, TOPK, FF), 1.0, 6.0, ((0, 8), (2, 64)))
    up_saved = centred(splits[2], (TOKENS, TOPK, FF), 1.0, 6.0, ((0, 8), (2, 64)))
    routing_keys = jax.random.split(jax.random.fold_in(splits[3], 1), TOKENS // GROUP_TOK)
    routing_turns = jax.random.permutation(jax.random.fold_in(splits[3], 3), TOKENS // GROUP_TOK)
    routing = jax.vmap(lambda own, number: routed_block(jax.random.fold_in(splits[3], 2), own, number, GROUP_TOK, EXPERTS, TOPK, CAP, 2))(routing_keys, routing_turns).reshape((TOKENS, TOPK))
    down_weight = centred(splits[4], (EXPERTS, D, FF), FF ** -0.5, 0.0625, ((0, 8), (2, 64)))
    momentum = centred(splits[5], (EXPERTS, D, FF), 10.0, 60.0, ((0, 8), (1, 64)))
    return dict(out_grad=out_grad, gate_saved=gate_saved, up_saved=up_saved, routing=routing, down_weight=down_weight, momentum=momentum)


beta_first = 0.9
beta_second = 0.99
step_rate = 0.01
decay_rate = 1.0
sign_width = 10.0


def slot_table(flat_route, experts, capacity):
    count_rows = flat_route.shape[0]
    onehot = (flat_route[:, None] == jnp.arange(experts, dtype=jnp.int32)[None, :]).astype(jnp.int32)
    before = jnp.cumsum(onehot, axis=0) - onehot
    place = jnp.sum(before * onehot, axis=1).astype(jnp.int32)
    table = jnp.full((experts, capacity), count_rows, jnp.int32)
    table = table.at[flat_route, place].set(jnp.arange(count_rows, dtype=jnp.int32))
    return table, jnp.sum(onehot, axis=0)


def reference(out_grad, gate_saved, up_saved, routing, down_weight, momentum):
    group_tok = GROUP_TOK
    count_rows = group_tok * TOPK
    gate_all = gate_saved.reshape(EXPERTS, count_rows, FF).astype(jnp.float32)
    up_all = up_saved.reshape(EXPERTS, count_rows, FF).astype(jnp.float32)
    sigma = jax.nn.sigmoid(gate_all)
    hidden = (gate_all * sigma * up_all).astype(jnp.bfloat16)
    grads = out_grad.reshape(EXPERTS, group_tok, D)
    route = routing.reshape(EXPERTS, count_rows).astype(jnp.int32)
    tables = []
    grads_pad = []
    hidden_pad = []
    for group in range(EXPERTS):
        tables.append(slot_table(route[group], EXPERTS, CAP)[0])
        grads_pad.append(jnp.concatenate([grads[group], jnp.zeros((1, D), jnp.bfloat16)], axis=0))
        hidden_pad.append(jnp.concatenate([hidden[group], jnp.zeros((1, FF), jnp.bfloat16)], axis=0))
    deriv = [jnp.zeros((count_rows + 1, FF), jnp.float32) for group in range(EXPERTS)]
    weights_out = []
    moments_out = []
    for expert in range(EXPERTS):
        carried = jnp.zeros((D, FF), jnp.bfloat16)
        for step in range(EXPERTS):
            group = (expert + step) % EXPERTS
            index = tables[group][expert]
            upstream = grads_pad[group][index // TOPK]
            picked = hidden_pad[group][index]
            deriv[group] = deriv[group].at[index].set(jnp.dot(upstream, down_weight[expert], preferred_element_type=jnp.float32))
            term = jnp.dot(upstream.T, picked, preferred_element_type=jnp.float32)
            carried = (carried.astype(jnp.float32) + term).astype(jnp.bfloat16)
        grad = carried.astype(jnp.float32)
        moment = momentum[expert].astype(jnp.float32)
        mix = beta_first * moment + (1.0 - beta_first) * grad
        weights_out.append(down_weight[expert].astype(jnp.float32) * (1.0 - step_rate * decay_rate) - step_rate * jnp.tanh(mix / sign_width))
        moments_out.append((beta_second * moment + (1.0 - beta_second) * grad).astype(jnp.bfloat16))
    dh = jnp.stack([deriv[group][:count_rows] for group in range(EXPERTS)])
    d_up = (dh * gate_all * sigma).astype(jnp.bfloat16).reshape(TOKENS, TOPK, FF)
    d_gate = (dh * up_all * sigma * (1.0 + gate_all * (1.0 - sigma))).astype(jnp.bfloat16).reshape(TOKENS, TOPK, FF)
    return d_gate, d_up, jnp.stack(weights_out), jnp.stack(moments_out)
```

```python
import functools

import jax
import jax.numpy as jnp
from jax import lax
from jax.experimental import pallas as pl
from jax.experimental.pallas import tpu as pltpu
from jax.sharding import PartitionSpec as P

beta_first = 0.9
beta_second = 0.99
step_rate = 0.01
decay_rate = 1.0
sign_width = 10.0

NZ, NX, NY, NLO, NHI = 16, 4, 4, 4, 4
CELLS = NX * NY
OWN = 7
RANGES = ((6, 4), (3, 3), (10, 3), (0, 3), (13, 3))
BF16, F32 = jnp.bfloat16, jnp.float32


def kernel(
    og_ref, w_ref, mt_ref, wr_ref, gr_ref, dr_ref,
    xb, x2, wp, ht, htq, ds, gf, gx, gy, gst,
    zs, zr, ags, agr, ws, wr, hs, hr, dsend, drecv, xs, xr, gs, grs, was, war,
):
    half = og_ref.shape[1]
    cols = w_ref.shape[1]
    expert, dp = lax.axis_index("expert"), lax.axis_index("dp")
    core, z_lo = expert % 2, expert // 2
    z_hi, x, y = dp // CELLS, (dp // NY) % NX, dp % NY
    cell = dp % CELLS
    z = z_hi * NLO + z_lo

    def at_z(zz):
        return {"expert": (zz % NLO) * 2 + core, "dp": (zz // NLO) * CELLS + cell}

    def at_cell(xx, yy):
        return {"expert": expert, "dp": z_hi * CELLS + xx * NY + yy}

    z_up, z_down = at_z((z + 1) % NZ), at_z((z + NZ - 1) % NZ)
    other = {"expert": z_lo * 2 + 1 - core, "dp": dp}

    def at_lo(lo):
        return {"expert": lo * 2 + core, "dp": dp}

    def at_dp(peer):
        return {"expert": expert, "dp": peer}

    def remote(src, dst, send, recv, device):
        return pltpu.make_async_remote_copy(
            src_ref=src, dst_ref=dst, send_sem=send, recv_sem=recv,
            device_id=device, device_id_type=pl.DeviceIdType.MESH,
        )

    barrier = pltpu.get_barrier_semaphore()

    def greet(device):
        pl.semaphore_signal(
            barrier, inc=1, device_id=device, device_id_type=pl.DeviceIdType.MESH
        )

    greet(z_up)
    greet(z_down)
    greet(other)
    for i in range(1, NLO):
        greet(at_lo((z_lo + i) % NLO))

    def greet_dp(i, carry):
        greet(at_dp((dp + i) % (NHI * CELLS)))
        return carry

    lax.fori_loop(1, NHI * CELLS, greet_dp, 0)

    xb[OWN, x, y] = og_ref[...]
    wp[:, pl.ds(pl.multiple_of(core * cols, cols), cols)] = w_ref[...]
    pl.semaphore_wait(barrier, 2 + 1 + NLO - 1 + NHI * CELLS - 1)

    def z_copy(q, step):
        device = z_down if step > 0 else z_up
        return remote(xb.at[q, x, y], xb.at[q + step, x, y], zs.at[q + step], zr.at[q + step], device)

    z_copies = []

    def z_start(q, step):
        copy = z_copy(q, step)
        copy.start()
        z_copies.append(copy)

    def z_step(k):
        z_copy(OWN + k - 1, 1).wait_recv()
        if OWN + k < NZ - 1:
            z_start(OWN + k, 1)
        if OWN - k >= 0:
            z_copy(OWN - k + 1, -1).wait_recv()
            if OWN - k > 0:
                z_start(OWN - k, -1)

    z_start(OWN, 1)
    z_start(OWN, -1)
    weight_copy = remote(
        w_ref, wp.at[:, pl.ds(pl.multiple_of(core * cols, cols), cols)], was.at[0], war.at[0], other
    )
    weight_copy.start()

    part = half // 2
    piece = part // 2

    def place(r, path, phase, source, first, width):
        slots = pl.ds(RANGES[r][0], RANGES[r][1])
        lanes = pl.ds(path * part + first, width)
        if phase == 0:
            return xb.at[slots, source, y, :, lanes] if path == 0 else xb.at[slots, x, source, :, lanes]
        return xb.at[slots, :, source, :, lanes] if path == 0 else xb.at[slots, source, :, :, lanes]

    def cell_copy(r, path, phase, kind):
        along_x = path == phase
        size = NX if along_x else NY
        mine = x if along_x else y
        right, left = (mine + 1) % size, (mine + size - 1) % size
        to = right if kind in (0, 2) else left
        device = at_cell(to, y) if along_x else at_cell(x, to)
        source = (mine, mine, left, right)[kind]
        first, width = ((0, part), (0, part), (0, piece), (piece, piece))[kind]
        ref = place(r, path, phase, source, first, width)
        return remote(ref, ref, ags.at[r, path, phase, kind], agr.at[r, path, phase, kind], device)

    cell_copies = []

    def cell_start(r, path, phase, kind):
        copy = cell_copy(r, path, phase, kind)
        copy.start()
        cell_copies.append(copy)

    def direct(r, phase):
        for path in range(2):
            cell_start(r, path, phase, 0)
            cell_start(r, path, phase, 1)

    def forward(r, phase):
        for path in range(2):
            for kind in (0, 1):
                cell_copy(r, path, phase, kind).wait_recv()
                cell_start(r, path, phase, kind + 2)

    def arrived(r, phase):
        for path in range(2):
            for kind in (2, 3):
                cell_copy(r, path, phase, kind).wait_recv()

    def turn(r):
        arrived(r, 0)
        direct(r, 1)

    rows = wr_ref.shape[0]
    my_lanes = pl.ds(pl.multiple_of(dp * cols, cols), cols)

    def weight_to(peer):
        src = w_ref.at[pl.ds(pl.multiple_of(peer * rows, rows), rows), :]
        return remote(src, wr_ref.at[:, my_lanes], ws.at[0], wr.at[0], at_dp(peer))

    def send_weight(i, carry):
        weight_to((dp + i) % (NHI * CELLS)).start()
        return carry

    def send_weights():
        pltpu.make_async_copy(
            w_ref.at[pl.ds(pl.multiple_of(dp * rows, rows), rows), :], wr_ref.at[:, my_lanes], wr.at[0]
        ).start()
        lax.fori_loop(1, NHI * CELLS, send_weight, 0)

    tokens = mt_ref.shape[2]

    def hidden_lanes(lo):
        return ht.at[:, pl.ds(pl.multiple_of(lo * tokens, tokens), tokens)]

    def send_hidden():
        pltpu.make_async_copy(mt_ref.at[z_lo], hidden_lanes(z_lo), hr.at[0]).start()
        for i in range(1, NLO):
            lo = (z_lo + i) % NLO
            remote(mt_ref.at[lo], hidden_lanes(z_lo), hs.at[i - 1], hr.at[0], at_lo(lo)).start()

    block = CELLS * 8

    def unpack(q, carry):
        row = pl.multiple_of(q * block, block)
        for first in range(0, half, 256):
            wide = xb[q, :, :, :, first:first + 256].astype(F32).reshape(CELLS, 16, 256)
            x2[pl.ds(row, block), first:first + 256] = wide[:, 0:8].reshape(block, 256).astype(BF16)
            x2[pl.ds(row, block), half + first:half + first + 256] = (
                wide[:, 8:16].reshape(block, 256).astype(BF16)
            )
        return carry

    def backward(r):
        first, slots = RANGES[r]
        lax.fori_loop(first, first + slots, unpack, 0)
        low, high = first * block, (first + slots) * block
        ds[low:high, :] = jnp.dot(x2[low:high, :], wp[...], preferred_element_type=F32)
        for q in range(first, first + slots):
            zz = (z + q + NZ - OWN) % NZ
            src = ds.at[pl.ds(q * block, block), :]
            dst = dr_ref.at[z_lo, pl.ds(pl.multiple_of((zz // NLO) * block, block), block), :]
            if (q - OWN) % NLO == 0:
                pltpu.make_async_copy(src, dst, drecv.at[0]).start()
            else:
                remote(src, dst, dsend.at[q], drecv.at[0], at_lo(zz % NLO)).start()

    z_step(1)
    z_step(2)
    direct(0, 0)
    z_step(3)
    forward(0, 0)
    z_step(4)
    direct(1, 0)
    turn(0)
    z_step(5)
    direct(2, 0)
    forward(1, 0)
    z_step(6)
    turn(1)
    forward(2, 0)
    z_step(7)
    direct(3, 0)
    turn(2)
    z_step(8)
    direct(4, 0)
    forward(3, 0)
    turn(3)
    forward(4, 0)
    turn(4)
    send_weights()
    send_hidden()
    forward(0, 1)
    weight_copy.wait_recv()
    forward(1, 1)
    arrived(0, 1)
    backward(0)
    forward(2, 1)
    arrived(1, 1)
    backward(1)
    forward(3, 1)
    arrived(2, 1)
    backward(2)
    forward(4, 1)
    arrived(3, 1)
    backward(3)
    arrived(4, 1)
    backward(4)

    pltpu.make_async_copy(ht, ht, hr.at[0]).wait()
    for q in range(NZ):
        zz = (z + q + NZ - OWN) % NZ
        lane = pl.multiple_of((zz % NLO) * tokens + (zz // NLO) * block, block)
        htq[:, q * block:(q + 1) * block] = ht[:, pl.ds(lane, block)]

    wide_piece = CELLS * rows
    mine = pl.ds(pl.multiple_of(core * cols, cols), cols)
    theirs = pl.ds(pl.multiple_of((1 - core) * cols, cols), cols)

    def exchange(s):
        return remote(gx.at[s], gy.at[s], xs.at[s], xr.at[s], other)

    def gradient(s):
        start = ((z_hi + s) % NHI) * wide_piece

        def tile(t, carry):
            lane = pl.multiple_of(start + t * 256, 256)
            gf[s, :, pl.ds(pl.multiple_of(t * 256, 256), 256)] = jnp.dot(
                htq[...], x2[:, pl.ds(lane, 256)], preferred_element_type=F32
            )
            return carry

        lax.fori_loop(0, wide_piece // 256, tile, 0)
        gx[s] = gf[s, theirs, :].astype(BF16)
        exchange(s).start()

    def gradient_to(s, c, src):
        peer = ((z_hi + s) % NHI) * CELLS + c
        return remote(src, gr_ref.at[:, my_lanes], gs.at[0], grs.at[0], at_dp(peer))

    def deliver(s):
        exchange(s).wait_recv()
        total = gf[s, mine, :] + gy[s].astype(F32)
        gst[s * wide_piece:(s + 1) * wide_piece, :] = total.T.astype(BF16)

        def rows_of(c):
            return gst.at[pl.ds(pl.multiple_of(s * wide_piece + c * rows, rows), rows), :]

        def send(i, carry):
            c = (cell + i) % CELLS
            gradient_to(s, c, rows_of(c)).start()
            return carry

        if s == 0:
            pltpu.make_async_copy(rows_of(cell), gr_ref.at[:, my_lanes], grs.at[0]).start()
        lax.fori_loop(1 if s == 0 else 0, CELLS, send, 0)

    for s in range(NHI):
        gradient(s)
        if s > 0:
            deliver(s - 1)
    deliver(NHI - 1)

    for copy in z_copies + cell_copies:
        copy.wait_send()
    weight_copy.wait_send()
    for i in range(1, NLO):
        lo = (z_lo + i) % NLO
        remote(mt_ref.at[lo], hidden_lanes(z_lo), hs.at[i - 1], hr.at[0], at_lo(lo)).wait_send()
    for q in range(NZ):
        if (q - OWN) % NLO != 0:
            src = ds.at[pl.ds(q * block, block), :]
            remote(src, src, dsend.at[q], drecv.at[0], other).wait_send()
    for s in range(NHI):
        exchange(s).wait_send()
    sent = w_ref.at[pl.ds(0, (NHI * CELLS - 1) * rows), :]
    pltpu.make_async_copy(sent, sent, ws.at[0]).wait()
    sent = gst.at[pl.ds(0, (NHI * CELLS - 1) * rows), :]
    pltpu.make_async_copy(sent, sent, gs.at[0]).wait()
    pltpu.make_async_copy(wr_ref, wr_ref, wr.at[0]).wait()
    pltpu.make_async_copy(dr_ref, dr_ref, drecv.at[0]).wait()
    pltpu.make_async_copy(gr_ref, gr_ref, grs.at[0]).wait()


def exchange_all(og, weight, hidden):
    half = og.shape[1]
    width, cols = weight.shape
    tokens = hidden.shape[2]
    rows = width // (NHI * CELLS)
    ff = cols * NHI * CELLS
    total = NZ * CELLS * 8
    any_space = pl.BlockSpec(memory_space=pl.ANY)
    vmem = pl.BlockSpec(memory_space=pltpu.VMEM)
    dma = pltpu.SemaphoreType.DMA
    return pl.pallas_call(
        kernel,
        out_shape=(
            jax.ShapeDtypeStruct((rows, ff), BF16),
            jax.ShapeDtypeStruct((rows, ff), BF16),
            jax.ShapeDtypeStruct((NLO, tokens, 2 * cols), F32),
        ),
        in_specs=[vmem] * 3,
        out_specs=(any_space,) * 3,
        scratch_shapes=[
            pltpu.VMEM((NZ, NX, NY, 16, half), BF16),
            pltpu.VMEM((total, width), BF16),
            pltpu.VMEM((width, 2 * cols), BF16),
            pltpu.VMEM((2 * cols, total), BF16),
            pltpu.VMEM((2 * cols, total), BF16),
            pltpu.VMEM((total, 2 * cols), F32),
            pltpu.VMEM((NHI, 2 * cols, width // NHI), F32),
            pltpu.VMEM((NHI, cols, width // NHI), BF16),
            pltpu.VMEM((NHI, cols, width // NHI), BF16),
            pltpu.VMEM((width, cols), BF16),
            dma((NZ,)), dma((NZ,)),
            dma((len(RANGES), 2, 2, 4)), dma((len(RANGES), 2, 2, 4)),
            dma((1,)), dma((1,)),
            dma((NLO - 1,)), dma((1,)),
            dma((NZ,)), dma((1,)),
            dma((NHI,)), dma((NHI,)),
            dma((1,)), dma((1,)),
            dma((1,)), dma((1,)),
        ],
        compiler_params=pltpu.CompilerParams(
            collective_id=0, has_side_effects=True, vmem_limit_bytes=56 * 1024 * 1024
        ),
    )(og, weight, hidden)


def body(out_grad, gate_saved, up_saved, routing, down_weight, momentum):
    group_tok, topk, cols = gate_saved.shape
    experts = lax.axis_size("expert")
    own_tok, width = out_grad.shape
    half = width // 2
    og = out_grad.reshape(own_tok, 2, half).transpose(1, 0, 2).reshape(2 * own_tok, half)
    gate = gate_saved.astype(F32)
    up = up_saved.astype(F32)
    sigma = jax.nn.sigmoid(gate)
    hidden = (gate * sigma * up).astype(BF16).transpose(1, 2, 0)
    ids = jnp.arange(experts, dtype=jnp.int32)[:, None, None]
    named = [routing[:, k][None, None, :] == ids for k in range(topk)]
    none = jnp.zeros((), BF16)
    sent = jnp.where(named[0], hidden[0][None], jnp.where(named[1], hidden[1][None], none))
    sent = sent.reshape(experts // 2, 2 * cols, group_tok)
    shard_weight, shard_grad, back = exchange_all(og, down_weight[0], sent)

    dh = jnp.zeros((group_tok, topk, cols), F32)
    for e in range(experts):
        one = back[e // 2, :, (e % 2) * cols:(e % 2 + 1) * cols]
        dh = jnp.where(routing[:, :, None] == e, one[:, None, :], dh)
    d_up = (dh * gate * sigma).astype(BF16)
    d_gate = (dh * up * sigma * (1.0 + gate * (1.0 - sigma))).astype(BF16)

    grad = shard_grad[None].astype(F32)
    moment = momentum.astype(F32)
    mix = beta_first * moment + (1.0 - beta_first) * grad
    new_weight = shard_weight[None].astype(F32) * (
        1.0 - step_rate * decay_rate
    ) - step_rate * jnp.tanh(mix / sign_width)
    new_momentum = (beta_second * moment + (1.0 - beta_second) * grad).astype(BF16)
    return (d_gate, d_up, new_weight, new_momentum)


def solution(mesh):
    placed = (
        P(("expert", "dp"), None),
        P("expert", None, "dp"),
        P("expert", None, "dp"),
        P("expert", None),
        P("expert", None, "dp"),
        P("expert", "dp", None),
    )
    return jax.shard_map(
        body,
        mesh=mesh,
        in_specs=placed,
        out_specs=(
            P("expert", None, "dp"),
            P("expert", None, "dp"),
            P("expert", "dp", None),
            P("expert", "dp", None),
        ),
        check_vma=False,
    )
```

```python
import functools

import jax
import jax.numpy as jnp
from jax import lax
from jax.experimental import pallas as pl
from jax.experimental.pallas import tpu as pltpu
from jax.sharding import PartitionSpec as P

beta_first = 0.9
beta_second = 0.99
step_rate = 0.01
decay_rate = 1.0
sign_width = 10.0

NZ, NX, NY, NLO, NHI = 16, 4, 4, 4, 4
CELLS = NX * NY
PAIR = 4
SLOTS = NZ // 2
OWN = SLOTS // 2 - 1
RANGES = ((2, 4), (0, 2), (6, 2))
BF16, F32 = jnp.bfloat16, jnp.float32


def kernel(
    og_ref, w_ref, hid_ref, wr_ref, gr_ref, dr_ref,
    xb, x2, wp, ht, htq, mk, dn, ds, gf, gx, gy, gu, px, py, gst,
    zs, zr, ags, agr, ws, wr, hs, hr, dsend, drecv, xs, xr, ps, pr, gs, grs, was, war,
):
    half = og_ref.shape[1]
    cols = w_ref.shape[1]
    expert, dp = lax.axis_index("expert"), lax.axis_index("dp")
    core, z_lo = expert % 2, expert // 2
    z_hi, x, y = dp // CELLS, (dp // NY) % NX, dp % NY
    cell = dp % CELLS
    z = z_hi * NLO + z_lo
    side, pair = z_lo % 2, z_lo // 2
    beside = pair * 2 + 1 - side
    across = (z_lo + 2) % NLO

    def at_z(zz):
        return {"expert": (zz % NLO) * 2 + core, "dp": (zz // NLO) * CELLS + cell}

    def at_cell(xx, yy):
        return {"expert": expert, "dp": z_hi * CELLS + xx * NY + yy}

    def at_lo(lo):
        return {"expert": lo * 2 + core, "dp": dp}

    def at_dp(peer):
        return {"expert": expert, "dp": peer}

    z_up, z_down = at_z((z + 2) % NZ), at_z((z + NZ - 2) % NZ)
    other = {"expert": z_lo * 2 + 1 - core, "dp": dp}

    def remote(src, dst, send, recv, device):
        return pltpu.make_async_remote_copy(
            src_ref=src, dst_ref=dst, send_sem=send, recv_sem=recv,
            device_id=device, device_id_type=pl.DeviceIdType.MESH,
        )

    barrier = pltpu.get_barrier_semaphore()

    def greet(device):
        pl.semaphore_signal(
            barrier, inc=1, device_id=device, device_id_type=pl.DeviceIdType.MESH
        )

    for device in (z_up, z_down, other, at_lo(beside), at_lo(across)):
        greet(device)

    def greet_dp(i, carry):
        greet(at_dp((dp + i) % (NHI * CELLS)))
        return carry

    lax.fori_loop(1, NHI * CELLS, greet_dp, 0)

    def expert_lanes(s, c):
        return pl.ds(pl.multiple_of((s * 2 + c) * cols, cols), cols)

    xb[OWN, x, y] = og_ref[...]
    wp[:, expert_lanes(side, core)] = w_ref[...]
    ht[0] = hid_ref[...]
    pl.semaphore_wait(barrier, 5 + NHI * CELLS - 1)

    def z_copy(q, step):
        device = z_down if step > 0 else z_up
        return remote(xb.at[q, x, y], xb.at[q + step, x, y], zs.at[q + step], zr.at[q + step], device)

    sends = []

    def start(copy):
        copy.start()
        sends.append(copy)

    def z_step(k):
        z_copy(OWN + k - 1, 1).wait_recv()
        if OWN + k < SLOTS - 1:
            start(z_copy(OWN + k, 1))
        if OWN - k >= 0:
            z_copy(OWN - k + 1, -1).wait_recv()
            if OWN - k > 0:
                start(z_copy(OWN - k, -1))

    start(z_copy(OWN, 1))
    start(z_copy(OWN, -1))

    own_weight = wp.at[:, expert_lanes(side, core)]
    to_core = remote(w_ref, own_weight, was.at[0], war.at[0], other)
    to_beside = remote(w_ref, own_weight, was.at[1], war.at[1], at_lo(beside))
    from_beside = wp.at[:, expert_lanes(1 - side, core)]
    relay = remote(from_beside, from_beside, was.at[2], war.at[2], other)
    start(to_core)
    start(to_beside)

    hidden_copy = remote(hid_ref, ht.at[1], hs.at[0], hr.at[0], at_lo(across))
    start(hidden_copy)

    part = half // 2
    piece = part // 2

    def place(r, path, phase, source, first, width):
        slots = pl.ds(RANGES[r][0], RANGES[r][1])
        lanes = pl.ds(path * part + first, width)
        if phase == 0:
            return xb.at[slots, source, y, :, lanes] if path == 0 else xb.at[slots, x, source, :, lanes]
        return xb.at[slots, :, source, :, lanes] if path == 0 else xb.at[slots, source, :, :, lanes]

    def cell_copy(r, path, phase, kind):
        along_x = path == phase
        size = NX if along_x else NY
        mine = x if along_x else y
        right, left = (mine + 1) % size, (mine + size - 1) % size
        to = right if kind in (0, 2) else left
        device = at_cell(to, y) if along_x else at_cell(x, to)
        source = (mine, mine, left, right)[kind]
        first, width = ((0, part), (0, part), (0, piece), (piece, piece))[kind]
        ref = place(r, path, phase, source, first, width)
        return remote(ref, ref, ags.at[r, path, phase, kind], agr.at[r, path, phase, kind], device)

    def direct(r, phase):
        for path in range(2):
            start(cell_copy(r, path, phase, 0))
            start(cell_copy(r, path, phase, 1))

    def forward(r, phase):
        for path in range(2):
            for kind in (0, 1):
                cell_copy(r, path, phase, kind).wait_recv()
                start(cell_copy(r, path, phase, kind + 2))

    def arrived(r, phase):
        for path in range(2):
            for kind in (2, 3):
                cell_copy(r, path, phase, kind).wait_recv()

    def turn(r):
        arrived(r, 0)
        direct(r, 1)

    rows = wr_ref.shape[0]
    my_lanes = pl.ds(pl.multiple_of(dp * cols, cols), cols)

    def send_weight(i, carry):
        peer = (dp + i) % (NHI * CELLS)
        src = w_ref.at[pl.ds(pl.multiple_of(peer * rows, rows), rows), :]
        remote(src, wr_ref.at[:, my_lanes], ws.at[0], wr.at[0], at_dp(peer)).start()
        return carry

    def send_weights():
        pltpu.make_async_copy(
            w_ref.at[pl.ds(pl.multiple_of(dp * rows, rows), rows), :], wr_ref.at[:, my_lanes], wr.at[0]
        ).start()
        lax.fori_loop(1, NHI * CELLS, send_weight, 0)

    block = CELLS * 8
    tokens = dr_ref.shape[1]

    def token_lane(q):
        return pl.multiple_of(((z + 2 * (q + SLOTS - OWN)) % NZ) // NLO * block, block)

    def unpack_hidden(q):
        lane = token_lane(q)
        which = (q - OWN) % 2
        named = ht[which, 2 * cols:2 * cols + 16, pl.ds(lane, block)].astype(F32)
        first = ht[which, 0:cols, pl.ds(lane, block)].astype(F32)
        second = ht[which, cols:2 * cols, pl.ds(lane, block)].astype(F32)
        hits = []
        for e in range(PAIR):
            index = (pair * PAIR + e).astype(F32)
            one = jnp.where(named[0:1] == index, 1.0, 0.0)
            two = jnp.where(named[1:2] == index, 1.0, 0.0)
            hits.append((one, two))
            htq[e * cols:(e + 1) * cols, q * block:(q + 1) * block] = (one * first + two * second).astype(BF16)
        for k in range(2):
            for e in range(PAIR):
                mk[q, k, e] = jnp.broadcast_to(hits[e][k], (block, block)).T

    def unpack(q, carry):
        row = pl.multiple_of(q * block, block)
        for first in range(0, half, 256):
            wide = xb[q, :, :, :, first:first + 256].astype(F32).reshape(CELLS, 16, 256)
            x2[pl.ds(row, block), first:first + 256] = wide[:, 0:8].reshape(block, 256).astype(BF16)
            x2[pl.ds(row, block), half + first:half + first + 256] = (
                wide[:, 8:16].reshape(block, 256).astype(BF16)
            )
        return carry

    def dh_copy(q):
        src = ds.at[pl.ds(q * block, block), :]
        lane = token_lane(q)
        if (q - OWN) % 2 == 0:
            return pltpu.make_async_copy(src, dr_ref.at[0, pl.ds(lane, block), :], drecv.at[0])
        return remote(src, dr_ref.at[1, pl.ds(lane, block), :], dsend.at[q], drecv.at[0], at_lo(across))

    def backward(r):
        first, slots = RANGES[r]
        lax.fori_loop(first, first + slots, unpack, 0)
        low, high = first * block, (first + slots) * block
        dn[low:high, :] = jnp.dot(x2[low:high, :], wp[...], preferred_element_type=F32)
        for q in range(first, first + slots):
            unpack_hidden(q)
            at = slice(q * block, (q + 1) * block)
            for k in range(2):
                picked = mk[q, k, 0] * dn[at, 0:cols]
                for e in range(1, PAIR):
                    picked += mk[q, k, e] * dn[at, e * cols:(e + 1) * cols]
                ds[at, k * cols:(k + 1) * cols] = picked
            dh_copy(q).start()

    z_step(1)
    z_step(2)
    direct(0, 0)
    z_step(3)
    direct(1, 0)
    forward(0, 0)
    z_step(4)
    direct(2, 0)
    turn(0)
    forward(1, 0)
    forward(2, 0)
    turn(1)
    turn(2)
    send_weights()
    to_beside.wait_recv()
    start(relay)
    hidden_copy.wait_recv()
    forward(0, 1)
    forward(1, 1)
    arrived(0, 1)
    to_core.wait_recv()
    relay.wait_recv()
    backward(0)
    forward(2, 1)
    arrived(1, 1)
    backward(1)
    arrived(2, 1)
    backward(2)

    wide_piece = CELLS * rows

    def expert_rows(s, c):
        return expert_lanes(s, c)

    def over_chip(s):
        return remote(gx.at[s], gy.at[s], xs.at[s], xr.at[s], other)

    def over_pair(s):
        return remote(px.at[s], py.at[s], ps.at[s], pr.at[s], at_lo(beside))

    def gradient(s):
        begin = ((z_hi + s) % NHI) * wide_piece

        def tile(t, carry):
            lane = pl.multiple_of(begin + t * 256, 256)
            gf[s, :, pl.ds(pl.multiple_of(t * 256, 256), 256)] = jnp.dot(
                htq[...], x2[:, pl.ds(lane, 256)], preferred_element_type=F32
            )
            return carry

        lax.fori_loop(0, wide_piece // 256, tile, 0)
        gx[s, 0] = gf[s, expert_rows(side, 1 - core), :].astype(BF16)
        gx[s, 1] = gf[s, expert_rows(1 - side, 1 - core), :].astype(BF16)
        start(over_chip(s))

    def sum_chip(s):
        over_chip(s).wait_recv()
        px[s] = (gf[s, expert_rows(1 - side, core), :] + gy[s, 1].astype(F32)).astype(BF16)
        start(over_pair(s))
        gu[s] = gf[s, expert_rows(side, core), :] + gy[s, 0].astype(F32)

    def deliver(s):
        over_pair(s).wait_recv()
        total = gu[s] + py[s].astype(F32)
        gst[s * wide_piece:(s + 1) * wide_piece, :] = total.T.astype(BF16)

        def rows_of(c):
            return gst.at[pl.ds(pl.multiple_of(s * wide_piece + c * rows, rows), rows), :]

        def send(i, carry):
            c = (cell + i) % CELLS
            peer = ((z_hi + s) % NHI) * CELLS + c
            remote(rows_of(c), gr_ref.at[:, my_lanes], gs.at[0], grs.at[0], at_dp(peer)).start()
            return carry

        if s == 0:
            pltpu.make_async_copy(rows_of(cell), gr_ref.at[:, my_lanes], grs.at[0]).start()
        lax.fori_loop(1 if s == 0 else 0, CELLS, send, 0)

    for s in range(NHI + 2):
        if s < NHI:
            gradient(s)
        if 0 < s < NHI + 1:
            sum_chip(s - 1)
        if s > 1:
            deliver(s - 2)

    for copy in sends:
        copy.wait_send()
    for q in range(SLOTS):
        if (q - OWN) % 2 != 0:
            dh_copy(q).wait_send()
    sent = w_ref.at[pl.ds(0, (NHI * CELLS - 1) * rows), :]
    pltpu.make_async_copy(sent, sent, ws.at[0]).wait()
    sent = gst.at[pl.ds(0, (NHI * CELLS - 1) * rows), :]
    pltpu.make_async_copy(sent, sent, gs.at[0]).wait()
    pltpu.make_async_copy(wr_ref, wr_ref, wr.at[0]).wait()
    pltpu.make_async_copy(dr_ref, dr_ref, drecv.at[0]).wait()
    pltpu.make_async_copy(gr_ref, gr_ref, grs.at[0]).wait()


def exchange_all(og, weight, hidden):
    half = og.shape[1]
    width, cols = weight.shape
    tokens = hidden.shape[1]
    rows = width // (NHI * CELLS)
    ff = cols * NHI * CELLS
    total = SLOTS * CELLS * 8
    piece = width // NHI
    any_space = pl.BlockSpec(memory_space=pl.ANY)
    vmem = pl.BlockSpec(memory_space=pltpu.VMEM)
    dma = pltpu.SemaphoreType.DMA
    ranges = len(RANGES)
    return pl.pallas_call(
        kernel,
        out_shape=(
            jax.ShapeDtypeStruct((rows, ff), BF16),
            jax.ShapeDtypeStruct((rows, ff), BF16),
            jax.ShapeDtypeStruct((2, tokens, 2 * cols), F32),
        ),
        in_specs=[vmem] * 3,
        out_specs=(any_space,) * 3,
        scratch_shapes=[
            pltpu.VMEM((SLOTS, NX, NY, 16, half), BF16),
            pltpu.VMEM((total, width), BF16),
            pltpu.VMEM((width, PAIR * cols), BF16),
            pltpu.VMEM((2, 2 * cols + 16, tokens), BF16),
            pltpu.VMEM((PAIR * cols, total), BF16),
            pltpu.VMEM((SLOTS, 2, PAIR, CELLS * 8, cols), F32),
            pltpu.VMEM((total, PAIR * cols), F32),
            pltpu.VMEM((total, 2 * cols), F32),
            pltpu.VMEM((NHI, PAIR * cols, piece), F32),
            pltpu.VMEM((NHI, 2, cols, piece), BF16),
            pltpu.VMEM((NHI, 2, cols, piece), BF16),
            pltpu.VMEM((NHI, cols, piece), F32),
            pltpu.VMEM((NHI, cols, piece), BF16),
            pltpu.VMEM((NHI, cols, piece), BF16),
            pltpu.VMEM((width, cols), BF16),
            dma((SLOTS,)), dma((SLOTS,)),
            dma((ranges, 2, 2, 4)), dma((ranges, 2, 2, 4)),
            dma((1,)), dma((1,)),
            dma((1,)), dma((1,)),
            dma((SLOTS,)), dma((1,)),
            dma((NHI,)), dma((NHI,)),
            dma((NHI,)), dma((NHI,)),
            dma((1,)), dma((1,)),
            dma((3,)), dma((3,)),
        ],
        compiler_params=pltpu.CompilerParams(
            collective_id=0, has_side_effects=True, vmem_limit_bytes=56 * 1024 * 1024
        ),
    )(og, weight, hidden)


def body(out_grad, gate_saved, up_saved, routing, down_weight, momentum):
    group_tok, topk, cols = gate_saved.shape
    own_tok, width = out_grad.shape
    half = width // 2
    og = out_grad.reshape(own_tok, 2, half).transpose(1, 0, 2).reshape(2 * own_tok, half)
    gate = gate_saved.astype(F32)
    up = up_saved.astype(F32)
    sigma = jax.nn.sigmoid(gate)
    hidden = (gate * sigma * up).astype(BF16).transpose(1, 2, 0)
    named = jnp.zeros((16, group_tok), BF16).at[:topk].set(routing.T.astype(BF16))
    sent = jnp.concatenate([hidden.reshape(topk * cols, group_tok), named], axis=0)
    shard_weight, shard_grad, back = exchange_all(og, down_weight[0], sent)
    dh = (back[0] + back[1]).reshape(group_tok, topk, cols)
    d_up = (dh * gate * sigma).astype(BF16)
    d_gate = (dh * up * sigma * (1.0 + gate * (1.0 - sigma))).astype(BF16)

    grad = shard_grad[None].astype(F32)
    moment = momentum.astype(F32)
    mix = beta_first * moment + (1.0 - beta_first) * grad
    new_weight = shard_weight[None].astype(F32) * (
        1.0 - step_rate * decay_rate
    ) - step_rate * jnp.tanh(mix / sign_width)
    new_momentum = (beta_second * moment + (1.0 - beta_second) * grad).astype(BF16)
    return (d_gate, d_up, new_weight, new_momentum)


def solution(mesh):
    placed = (
        P(("expert", "dp"), None),
        P("expert", None, "dp"),
        P("expert", None, "dp"),
        P("expert", None),
        P("expert", None, "dp"),
        P("expert", "dp", None),
    )
    return jax.shard_map(
        body,
        mesh=mesh,
        in_specs=placed,
        out_specs=(
            P("expert", None, "dp"),
            P("expert", None, "dp"),
            P("expert", "dp", None),
            P("expert", "dp", None),
        ),
        check_vma=False,
    )
```

```python
import functools

import jax
import jax.numpy as jnp
from jax import lax
from jax.experimental import pallas as pl
from jax.experimental.pallas import tpu as pltpu
from jax.sharding import PartitionSpec as P

beta_first = 0.9
beta_second = 0.99
step_rate = 0.01
decay_rate = 1.0
sign_width = 10.0

NZ, NX, NY, NLO, NHI = 16, 4, 4, 4, 4
CELLS = NX * NY
PAIR = 4
SLOTS = NZ // 2
OWN = SLOTS // 2 - 1
RANGES = ((2, 4), (0, 2), (6, 2))
BF16, F32 = jnp.bfloat16, jnp.float32


def kernel(
    og_ref, w_ref, hid_ref, wr_ref, gr_ref, dr_ref,
    xb, x2, wp, ht, htq, mk, dn, ds, gf, gx, gy, gu, px, py, gst,
    zs, zr, ags, agr, ws, wr, hs, hr, dsend, drecv, xs, xr, ps, pr, gs, grs, was, war,
):
    half = og_ref.shape[1]
    cols = w_ref.shape[1]
    expert, dp = lax.axis_index("expert"), lax.axis_index("dp")
    core, z_lo = expert % 2, expert // 2
    z_hi, x, y = dp // CELLS, (dp // NY) % NX, dp % NY
    cell = dp % CELLS
    z = z_hi * NLO + z_lo
    side, pair = z_lo % 2, z_lo // 2
    beside = pair * 2 + 1 - side
    across = (z_lo + 2) % NLO

    def at_z(zz):
        return {"expert": (zz % NLO) * 2 + core, "dp": (zz // NLO) * CELLS + cell}

    def at_cell(xx, yy):
        return {"expert": expert, "dp": z_hi * CELLS + xx * NY + yy}

    def at_lo(lo):
        return {"expert": lo * 2 + core, "dp": dp}

    away = (z_hi + NHI - 1 + 2 * side) % NHI
    toward = (z_hi + 1 + 2 * side) % NHI
    far = (z_hi + 2) % NHI

    def owner(lo, hi, c):
        return {"expert": lo * 2 + core, "dp": hi * CELLS + c}

    z_up, z_down = at_z((z + 2) % NZ), at_z((z + NZ - 2) % NZ)
    other = {"expert": z_lo * 2 + 1 - core, "dp": dp}

    def remote(src, dst, send, recv, device):
        return pltpu.make_async_remote_copy(
            src_ref=src, dst_ref=dst, send_sem=send, recv_sem=recv,
            device_id=device, device_id_type=pl.DeviceIdType.MESH,
        )

    barrier = pltpu.get_barrier_semaphore()

    def greet(device):
        pl.semaphore_signal(
            barrier, inc=1, device_id=device, device_id_type=pl.DeviceIdType.MESH
        )

    for device in (z_up, z_down, other, at_lo(beside), at_lo(across)):
        greet(device)

    def greet_cells(i, carry):
        c = (cell + i) % CELLS
        greet(owner(z_lo, toward, c))
        greet(owner(beside, away, c))
        greet(owner(beside, far, c))
        return carry

    def greet_near(i, carry):
        greet(owner(z_lo, z_hi, (cell + i) % CELLS))
        return carry

    lax.fori_loop(0, CELLS, greet_cells, 0)
    lax.fori_loop(1, CELLS, greet_near, 0)

    def expert_lanes(s, c):
        return pl.ds(pl.multiple_of((s * 2 + c) * cols, cols), cols)

    xb[OWN, x, y] = og_ref[...]
    wp[:, expert_lanes(side, core)] = w_ref[...]
    ht[0] = hid_ref[...]
    pl.semaphore_wait(barrier, 5 + NHI * CELLS - 1)

    def z_copy(q, step):
        device = z_down if step > 0 else z_up
        return remote(xb.at[q, x, y], xb.at[q + step, x, y], zs.at[q + step], zr.at[q + step], device)

    sends = []

    def start(copy):
        copy.start()
        sends.append(copy)

    def z_step(k):
        z_copy(OWN + k - 1, 1).wait_recv()
        if OWN + k < SLOTS - 1:
            start(z_copy(OWN + k, 1))
        if OWN - k >= 0:
            z_copy(OWN - k + 1, -1).wait_recv()
            if OWN - k > 0:
                start(z_copy(OWN - k, -1))

    start(z_copy(OWN, 1))
    start(z_copy(OWN, -1))

    own_weight = wp.at[:, expert_lanes(side, core)]
    to_core = remote(w_ref, own_weight, was.at[0], war.at[0], other)
    to_beside = remote(w_ref, own_weight, was.at[1], war.at[1], at_lo(beside))
    from_beside = wp.at[:, expert_lanes(1 - side, core)]
    relay = remote(from_beside, from_beside, was.at[2], war.at[2], other)
    start(to_core)

    hidden_copy = remote(hid_ref, ht.at[1], hs.at[0], hr.at[0], at_lo(across))

    part = half // 2
    piece = part // 2

    def place(r, path, phase, source, first, width):
        slots = pl.ds(RANGES[r][0], RANGES[r][1])
        lanes = pl.ds(path * part + first, width)
        if phase == 0:
            return xb.at[slots, source, y, :, lanes] if path == 0 else xb.at[slots, x, source, :, lanes]
        return xb.at[slots, :, source, :, lanes] if path == 0 else xb.at[slots, source, :, :, lanes]

    def cell_copy(r, path, phase, kind):
        along_x = path == phase
        size = NX if along_x else NY
        mine = x if along_x else y
        right, left = (mine + 1) % size, (mine + size - 1) % size
        to = right if kind in (0, 2) else left
        device = at_cell(to, y) if along_x else at_cell(x, to)
        source = (mine, mine, left, right)[kind]
        first, width = ((0, part), (0, part), (0, piece), (piece, piece))[kind]
        ref = place(r, path, phase, source, first, width)
        return remote(ref, ref, ags.at[r, path, phase, kind], agr.at[r, path, phase, kind], device)

    def direct(r, phase):
        for path in range(2):
            start(cell_copy(r, path, phase, 0))
            start(cell_copy(r, path, phase, 1))

    def forward(r, phase):
        for path in range(2):
            for kind in (0, 1):
                cell_copy(r, path, phase, kind).wait_recv()
                start(cell_copy(r, path, phase, kind + 2))

    def arrived(r, phase):
        for path in range(2):
            for kind in (2, 3):
                cell_copy(r, path, phase, kind).wait_recv()

    def turn(r):
        arrived(r, 0)
        direct(r, 1)

    rows = wr_ref.shape[0]
    my_lanes = pl.ds(pl.multiple_of(dp * cols, cols), cols)

    def weight_rows(s, hi, c):
        row = pl.multiple_of((hi * CELLS + c) * rows, rows)
        return wp.at[pl.ds(row, rows), expert_lanes(s, core)]

    def send_weight(lo, s, hi, c):
        remote(weight_rows(s, hi, c), wr_ref.at[:, my_lanes], ws.at[0], wr.at[0], owner(lo, hi, c)).start()

    def send_own(i, carry):
        send_weight(z_lo, side, away, (cell + i) % CELLS)
        return carry

    def send_near(i, carry):
        send_weight(z_lo, side, z_hi, (cell + i) % CELLS)
        return carry

    def send_beside(i, carry):
        send_weight(beside, 1 - side, far, (cell + i) % CELLS)
        send_weight(beside, 1 - side, away, (cell + i) % CELLS)
        return carry

    def send_weights():
        pltpu.make_async_copy(weight_rows(side, z_hi, cell), wr_ref.at[:, my_lanes], wr.at[0]).start()
        lax.fori_loop(0, CELLS, send_own, 0)
        lax.fori_loop(1, CELLS, send_near, 0)

    block = CELLS * 8
    tokens = dr_ref.shape[1]

    def token_lane(q):
        return pl.multiple_of(((z + 2 * (q + SLOTS - OWN)) % NZ) // NLO * block, block)

    def unpack_hidden(q):
        lane = token_lane(q)
        which = (q - OWN) % 2
        named = ht[which, 2 * cols:2 * cols + 16, pl.ds(lane, block)].astype(F32)
        first = ht[which, 0:cols, pl.ds(lane, block)].astype(F32)
        second = ht[which, cols:2 * cols, pl.ds(lane, block)].astype(F32)
        hits = []
        for e in range(PAIR):
            index = (pair * PAIR + e).astype(F32)
            one = jnp.where(named[0:1] == index, 1.0, 0.0)
            two = jnp.where(named[1:2] == index, 1.0, 0.0)
            hits.append((one, two))
            htq[e * cols:(e + 1) * cols, q * block:(q + 1) * block] = (one * first + two * second).astype(BF16)
        for k in range(2):
            for e in range(PAIR):
                mk[q, k, e] = jnp.broadcast_to(hits[e][k], (block, block)).T

    def unpack(q, carry):
        row = pl.multiple_of(q * block, block)
        for first in range(0, half, 256):
            wide = xb[q, :, :, :, first:first + 256].astype(F32).reshape(CELLS, 16, 256)
            x2[pl.ds(row, block), first:first + 256] = wide[:, 0:8].reshape(block, 256).astype(BF16)
            x2[pl.ds(row, block), half + first:half + first + 256] = (
                wide[:, 8:16].reshape(block, 256).astype(BF16)
            )
        return carry

    def dh_copy(q):
        src = ds.at[pl.ds(q * block, block), :]
        lane = token_lane(q)
        if (q - OWN) % 2 == 0:
            return pltpu.make_async_copy(src, dr_ref.at[0, pl.ds(lane, block), :], drecv.at[0])
        return remote(src, dr_ref.at[1, pl.ds(lane, block), :], dsend.at[q], drecv.at[0], at_lo(across))

    def backward(r):
        first, slots = RANGES[r]
        lax.fori_loop(first, first + slots, unpack, 0)
        low, high = first * block, (first + slots) * block
        dn[low:high, :] = jnp.dot(x2[low:high, :], wp[...], preferred_element_type=F32)
        for q in range(first, first + slots):
            unpack_hidden(q)
            at = slice(q * block, (q + 1) * block)
            for k in range(2):
                picked = mk[q, k, 0] * dn[at, 0:cols]
                for e in range(1, PAIR):
                    picked += mk[q, k, e] * dn[at, e * cols:(e + 1) * cols]
                ds[at, k * cols:(k + 1) * cols] = picked

    z_step(1)
    z_step(2)
    direct(0, 0)
    z_step(3)
    direct(1, 0)
    forward(0, 0)
    z_step(4)
    direct(2, 0)
    start(to_beside)
    start(hidden_copy)
    send_weights()
    turn(0)
    forward(1, 0)
    forward(2, 0)
    turn(1)
    turn(2)
    to_beside.wait_recv()
    start(relay)
    hidden_copy.wait_recv()
    lax.fori_loop(0, CELLS, send_beside, 0)
    forward(0, 1)
    forward(1, 1)
    arrived(0, 1)
    to_core.wait_recv()
    relay.wait_recv()
    backward(0)
    forward(2, 1)
    arrived(1, 1)
    backward(1)
    arrived(2, 1)
    backward(2)

    wide_piece = CELLS * rows
    targets = (toward, far, z_hi, away)

    def over_chip(s):
        return remote(gx.at[s], gy.at[s], xs.at[s], xr.at[s], other)

    def over_pair(slot):
        return remote(px.at[slot], py.at[slot], ps.at[slot], pr.at[slot], at_lo(beside))

    def gradient(s):
        begin = targets[s] * wide_piece

        def tile(t, carry):
            lane = pl.multiple_of(begin + t * 256, 256)
            gf[s, :, pl.ds(pl.multiple_of(t * 256, 256), 256)] = jnp.dot(
                htq[...], x2[:, pl.ds(lane, 256)], preferred_element_type=F32
            )
            return carry

        lax.fori_loop(0, wide_piece // 256, tile, 0)
        gx[s, 0] = gf[s, expert_lanes(side, 1 - core), :].astype(BF16)
        gx[s, 1] = gf[s, expert_lanes(1 - side, 1 - core), :].astype(BF16)
        start(over_chip(s))

    def chip_sum(s, own):
        lanes = expert_lanes(side, core) if own else expert_lanes(1 - side, core)
        return gf[s, lanes, :] + gy[s, 0 if own else 1].astype(F32)

    def sum_chip(s):
        over_chip(s).wait_recv()
        if s == 0:
            px[0] = chip_sum(0, True).astype(BF16)
            start(over_pair(0))
            px[1] = chip_sum(0, False).astype(BF16)
            start(over_pair(1))
        elif s == 1:
            px[2] = chip_sum(1, True).astype(BF16)
            start(over_pair(2))
            gu[0] = chip_sum(1, False)
        elif s == 2:
            px[3] = chip_sum(2, False).astype(BF16)
            start(over_pair(3))
            gu[1] = chip_sum(2, True)
        else:
            gu[2] = chip_sum(3, True)
            gu[3] = chip_sum(3, False)

    def deliver(part_sum, slot, lo, hi, near):
        over_pair(slot).wait_recv()
        total = gu[part_sum] + py[slot].astype(F32)
        gst[part_sum * wide_piece:(part_sum + 1) * wide_piece, :] = total.T.astype(BF16)

        def rows_of(c):
            return gst.at[pl.ds(pl.multiple_of(part_sum * wide_piece + c * rows, rows), rows), :]

        def send(i, carry):
            c = (cell + i) % CELLS
            remote(rows_of(c), gr_ref.at[:, my_lanes], gs.at[0], grs.at[0], owner(lo, hi, c)).start()
            return carry

        if near:
            pltpu.make_async_copy(rows_of(cell), gr_ref.at[:, my_lanes], grs.at[0]).start()
        lax.fori_loop(1 if near else 0, CELLS, send, 0)

    gradient(1)
    gradient(0)
    sum_chip(1)
    sum_chip(0)
    for q in range(SLOTS):
        dh_copy(q).start()
    gradient(2)
    gradient(3)
    deliver(0, 2, beside, far, False)
    sum_chip(2)
    sum_chip(3)
    deliver(3, 0, beside, away, False)
    deliver(2, 1, z_lo, away, False)
    deliver(1, 3, z_lo, z_hi, True)

    for copy in sends:
        copy.wait_send()
    for q in range(SLOTS):
        if (q - OWN) % 2 != 0:
            dh_copy(q).wait_send()
    sent = w_ref.at[pl.ds(0, (NHI * CELLS - 1) * rows), :]
    pltpu.make_async_copy(sent, sent, ws.at[0]).wait()
    sent = gst.at[pl.ds(0, (NHI * CELLS - 1) * rows), :]
    pltpu.make_async_copy(sent, sent, gs.at[0]).wait()
    pltpu.make_async_copy(wr_ref, wr_ref, wr.at[0]).wait()
    pltpu.make_async_copy(dr_ref, dr_ref, drecv.at[0]).wait()
    pltpu.make_async_copy(gr_ref, gr_ref, grs.at[0]).wait()


def exchange_all(og, weight, hidden):
    half = og.shape[1]
    width, cols = weight.shape
    tokens = hidden.shape[1]
    rows = width // (NHI * CELLS)
    ff = cols * NHI * CELLS
    total = SLOTS * CELLS * 8
    piece = width // NHI
    any_space = pl.BlockSpec(memory_space=pl.ANY)
    vmem = pl.BlockSpec(memory_space=pltpu.VMEM)
    dma = pltpu.SemaphoreType.DMA
    ranges = len(RANGES)
    return pl.pallas_call(
        kernel,
        out_shape=(
            jax.ShapeDtypeStruct((rows, ff), BF16),
            jax.ShapeDtypeStruct((rows, ff), BF16),
            jax.ShapeDtypeStruct((2, tokens, 2 * cols), F32),
        ),
        in_specs=[vmem] * 3,
        out_specs=(any_space,) * 3,
        scratch_shapes=[
            pltpu.VMEM((SLOTS, NX, NY, 16, half), BF16),
            pltpu.VMEM((total, width), BF16),
            pltpu.VMEM((width, PAIR * cols), BF16),
            pltpu.VMEM((2, 2 * cols + 16, tokens), BF16),
            pltpu.VMEM((PAIR * cols, total), BF16),
            pltpu.VMEM((SLOTS, 2, PAIR, CELLS * 8, cols), F32),
            pltpu.VMEM((total, PAIR * cols), F32),
            pltpu.VMEM((total, 2 * cols), F32),
            pltpu.VMEM((NHI, PAIR * cols, piece), F32),
            pltpu.VMEM((NHI, 2, cols, piece), BF16),
            pltpu.VMEM((NHI, 2, cols, piece), BF16),
            pltpu.VMEM((NHI, cols, piece), F32),
            pltpu.VMEM((NHI, cols, piece), BF16),
            pltpu.VMEM((NHI, cols, piece), BF16),
            pltpu.VMEM((width, cols), BF16),
            dma((SLOTS,)), dma((SLOTS,)),
            dma((ranges, 2, 2, 4)), dma((ranges, 2, 2, 4)),
            dma((1,)), dma((1,)),
            dma((1,)), dma((1,)),
            dma((SLOTS,)), dma((1,)),
            dma((NHI,)), dma((NHI,)),
            dma((NHI,)), dma((NHI,)),
            dma((1,)), dma((1,)),
            dma((3,)), dma((3,)),
        ],
        compiler_params=pltpu.CompilerParams(
            collective_id=0, has_side_effects=True, vmem_limit_bytes=56 * 1024 * 1024
        ),
    )(og, weight, hidden)


def body(out_grad, gate_saved, up_saved, routing, down_weight, momentum):
    group_tok, topk, cols = gate_saved.shape
    own_tok, width = out_grad.shape
    half = width // 2
    og = out_grad.reshape(own_tok, 2, half).transpose(1, 0, 2).reshape(2 * own_tok, half)
    gate = gate_saved.astype(F32)
    up = up_saved.astype(F32)
    sigma = jax.nn.sigmoid(gate)
    hidden = (gate * sigma * up).astype(BF16).transpose(1, 2, 0)
    named = jnp.zeros((16, group_tok), BF16).at[:topk].set(routing.T.astype(BF16))
    sent = jnp.concatenate([hidden.reshape(topk * cols, group_tok), named], axis=0)
    shard_weight, shard_grad, back = exchange_all(og, down_weight[0], sent)
    dh = (back[0] + back[1]).reshape(group_tok, topk, cols)
    d_up = (dh * gate * sigma).astype(BF16)
    d_gate = (dh * up * sigma * (1.0 + gate * (1.0 - sigma))).astype(BF16)

    grad = shard_grad[None].astype(F32)
    moment = momentum.astype(F32)
    mix = beta_first * moment + (1.0 - beta_first) * grad
    new_weight = shard_weight[None].astype(F32) * (
        1.0 - step_rate * decay_rate
    ) - step_rate * jnp.tanh(mix / sign_width)
    new_momentum = (beta_second * moment + (1.0 - beta_second) * grad).astype(BF16)
    return (d_gate, d_up, new_weight, new_momentum)


def solution(mesh):
    placed = (
        P(("expert", "dp"), None),
        P("expert", None, "dp"),
        P("expert", None, "dp"),
        P("expert", None),
        P("expert", None, "dp"),
        P("expert", "dp", None),
    )
    return jax.shard_map(
        body,
        mesh=mesh,
        in_specs=placed,
        out_specs=(
            P("expert", None, "dp"),
            P("expert", None, "dp"),
            P("expert", "dp", None),
            P("expert", "dp", None),
        ),
        check_vma=False,
    )
```

```python
import functools

import jax
import jax.numpy as jnp
from jax import lax
from jax.experimental import pallas as pl
from jax.experimental.pallas import tpu as pltpu
from jax.sharding import PartitionSpec as P

beta_first = 0.9
beta_second = 0.99
step_rate = 0.01
decay_rate = 1.0
sign_width = 10.0

NZ, NX, NY, NLO, NHI = 16, 4, 4, 4, 4
CELLS = NX * NY
PAIR = 4
SLOTS = NZ // 2
OWN = SLOTS // 2 - 1
RANGES = ((2, 4), (0, 2), (6, 2))
BF16, F32 = jnp.bfloat16, jnp.float32


def kernel(
    og_ref, w_ref, gate_ref, up_ref, named_ref, wr_ref, gr_ref, dr_ref, da_ref,
    xb, x2, wp, hf, ht, htq, mk, dn, ds, gf, gx, gy, gu, px, py, gst,
    zs, zr, ags, agr, ws, wr, hs, hr, dsend, drecv, xs, xr, ps, pr, gs, grs, was, war,
    row_sem, plane_sem,
):
    half = og_ref.shape[1]
    cols = w_ref.shape[1]
    expert, dp = lax.axis_index("expert"), lax.axis_index("dp")
    core, z_lo = expert % 2, expert // 2
    z_hi, x, y = dp // CELLS, (dp // NY) % NX, dp % NY
    cell = dp % CELLS
    z = z_hi * NLO + z_lo
    side, pair = z_lo % 2, z_lo // 2
    beside = pair * 2 + 1 - side
    across = (z_lo + 2) % NLO

    def at_z(zz):
        return {"expert": (zz % NLO) * 2 + core, "dp": (zz // NLO) * CELLS + cell}

    def at_cell(xx, yy):
        return {"expert": expert, "dp": z_hi * CELLS + xx * NY + yy}

    def at_lo(lo):
        return {"expert": lo * 2 + core, "dp": dp}

    away = (z_hi + NHI - 1 + 2 * side) % NHI
    toward = (z_hi + 1 + 2 * side) % NHI
    far = (z_hi + 2) % NHI

    def owner(lo, hi, c):
        return {"expert": lo * 2 + core, "dp": hi * CELLS + c}

    z_up, z_down = at_z((z + 2) % NZ), at_z((z + NZ - 2) % NZ)
    other = {"expert": z_lo * 2 + 1 - core, "dp": dp}

    def remote(src, dst, send, recv, device):
        return pltpu.make_async_remote_copy(
            src_ref=src, dst_ref=dst, send_sem=send, recv_sem=recv,
            device_id=device, device_id_type=pl.DeviceIdType.MESH,
        )

    barrier = pltpu.get_barrier_semaphore()

    def greet(semaphore, device):
        pl.semaphore_signal(
            semaphore, inc=1, device_id=device, device_id_type=pl.DeviceIdType.MESH
        )

    column = [at_cell(x, (y + i) % NY) for i in range(1, NY)]
    levels = [owner(z_lo, (z_hi + i) % NHI, cell) for i in range(1, NHI)]
    levels += [owner(beside, (z_hi + i) % NHI, cell) for i in range(NHI)]
    nearby = [z_up, z_down, other, at_lo(across)]
    nearby += [at_cell((x + i) % NX, y) for i in range(1, NX)] + column + levels
    for device in nearby:
        greet(barrier, device)

    def expert_lanes(s, c):
        return pl.ds(pl.multiple_of((s * 2 + c) * cols, cols), cols)

    xb[OWN, x, y] = og_ref[...]
    wp[:, expert_lanes(side, core)] = w_ref[...]
    pl.semaphore_wait(barrier, len(nearby))

    def z_copy(q, step):
        device = z_down if step > 0 else z_up
        return remote(xb.at[q, x, y], xb.at[q + step, x, y], zs.at[q + step], zr.at[q + step], device)

    sends = []

    def start(copy):
        copy.start()
        sends.append(copy)

    def z_step(k):
        z_copy(OWN + k - 1, 1).wait_recv()
        if OWN + k < SLOTS - 1:
            start(z_copy(OWN + k, 1))
        if OWN - k >= 0:
            z_copy(OWN - k + 1, -1).wait_recv()
            if OWN - k > 0:
                start(z_copy(OWN - k, -1))

    start(z_copy(OWN, 1))
    start(z_copy(OWN, -1))

    own_weight = wp.at[:, expert_lanes(side, core)]
    to_core = remote(w_ref, own_weight, was.at[0], war.at[0], other)
    to_beside = remote(w_ref, own_weight, was.at[1], war.at[1], at_lo(beside))
    from_beside = wp.at[:, expert_lanes(1 - side, core)]
    relay = remote(from_beside, from_beside, was.at[2], war.at[2], other)
    start(to_core)
    for device in column:
        greet(row_sem, device)

    hidden_copy = remote(ht.at[0], ht.at[1], hs.at[0], hr.at[0], at_lo(across))

    part = half // 2
    piece = part // 2

    def place(r, path, phase, source, first, width):
        slots = pl.ds(RANGES[r][0], RANGES[r][1])
        lanes = pl.ds(path * part + first, width)
        if phase == 0:
            return xb.at[slots, source, y, :, lanes] if path == 0 else xb.at[slots, x, source, :, lanes]
        return xb.at[slots, :, source, :, lanes] if path == 0 else xb.at[slots, source, :, :, lanes]

    def cell_copy(r, path, phase, kind):
        along_x = path == phase
        size = NX if along_x else NY
        mine = x if along_x else y
        right, left = (mine + 1) % size, (mine + size - 1) % size
        to = right if kind in (0, 2) else left
        device = at_cell(to, y) if along_x else at_cell(x, to)
        source = (mine, mine, left, right)[kind]
        first, width = ((0, part), (0, part), (0, piece), (piece, piece))[kind]
        ref = place(r, path, phase, source, first, width)
        return remote(ref, ref, ags.at[r, path, phase, kind], agr.at[r, path, phase, kind], device)

    def direct(r, phase):
        for path in range(2):
            start(cell_copy(r, path, phase, 0))
            start(cell_copy(r, path, phase, 1))

    def forward(r, phase):
        for path in range(2):
            for kind in (0, 1):
                cell_copy(r, path, phase, kind).wait_recv()
                start(cell_copy(r, path, phase, kind + 2))

    def arrived(r, phase):
        for path in range(2):
            for kind in (2, 3):
                cell_copy(r, path, phase, kind).wait_recv()

    def turn(r):
        arrived(r, 0)
        direct(r, 1)

    rows = wr_ref.shape[0]
    my_lanes = pl.ds(pl.multiple_of(dp * cols, cols), cols)

    def weight_rows(s, hi, c):
        row = pl.multiple_of((hi * CELLS + c) * rows, rows)
        return wp.at[pl.ds(row, rows), expert_lanes(s, core)]

    def send_weight(lo, s, hi, c):
        remote(weight_rows(s, hi, c), wr_ref.at[:, my_lanes], ws.at[0], wr.at[0], owner(lo, hi, c)).start()

    def send_own(i, carry):
        send_weight(z_lo, side, away, (cell + i) % CELLS)
        return carry

    def send_near(i, carry):
        send_weight(z_lo, side, z_hi, (cell + i) % CELLS)
        return carry

    def send_beside(i, carry):
        send_weight(beside, 1 - side, far, (cell + i) % CELLS)
        send_weight(beside, 1 - side, away, (cell + i) % CELLS)
        return carry

    def send_weights():
        pltpu.make_async_copy(weight_rows(side, z_hi, cell), wr_ref.at[:, my_lanes], wr.at[0]).start()
        lax.fori_loop(0, CELLS, send_own, 0)
        lax.fori_loop(1, CELLS, send_near, 0)

    block = CELLS * 8
    tokens = named_ref.shape[1]

    def token_lane(q):
        return pl.multiple_of(((z + 2 * (q + SLOTS - OWN)) % NZ) // NLO * block, block)

    def unpack_hidden(q):
        lane = token_lane(q)
        which = (q - OWN) % 2
        named = ht[which, 2 * cols:2 * cols + 16, pl.ds(lane, block)].astype(F32)
        first = ht[which, 0:cols, pl.ds(lane, block)].astype(F32)
        second = ht[which, cols:2 * cols, pl.ds(lane, block)].astype(F32)
        hits = []
        for e in range(PAIR):
            index = (pair * PAIR + e).astype(F32)
            one = jnp.where(named[0:1] == index, 1.0, 0.0)
            two = jnp.where(named[1:2] == index, 1.0, 0.0)
            hits.append((one, two))
            htq[e * cols:(e + 1) * cols, q * block:(q + 1) * block] = (one * first + two * second).astype(BF16)
        for k in range(2):
            for e in range(PAIR):
                mk[q, k, e] = jnp.broadcast_to(hits[e][k], (block, block)).T

    def unpack(q, carry):
        row = pl.multiple_of(q * block, block)
        for first in range(0, half, 256):
            wide = xb[q, :, :, :, first:first + 256].astype(F32).reshape(CELLS, 16, 256)
            x2[pl.ds(row, block), first:first + 256] = wide[:, 0:8].reshape(block, 256).astype(BF16)
            x2[pl.ds(row, block), half + first:half + first + 256] = (
                wide[:, 8:16].reshape(block, 256).astype(BF16)
            )
        return carry

    def dh_copy(q):
        src = ds.at[pl.ds(q * 2 * block, 2 * block), :]
        row = pl.multiple_of(2 * token_lane(q), 2 * block)
        if (q - OWN) % 2 == 0:
            return pltpu.make_async_copy(src, dr_ref.at[pl.ds(row, 2 * block), :], drecv.at[0])
        return remote(src, da_ref.at[pl.ds(row, 2 * block), :], dsend.at[q], drecv.at[1], at_lo(across))

    def backward(r):
        first, slots = RANGES[r]
        lax.fori_loop(first, first + slots, unpack, 0)
        low, high = first * block, (first + slots) * block
        dn[low:high, :] = jnp.dot(x2[low:high, :], wp[...], preferred_element_type=F32)
        for q in range(first, first + slots):
            unpack_hidden(q)
            at = slice(q * block, (q + 1) * block)
            for k in range(2):
                picked = mk[q, k, 0] * dn[at, 0:cols]
                for e in range(1, PAIR):
                    picked += mk[q, k, e] * dn[at, e * cols:(e + 1) * cols]
                ds[pl.ds(q * 2 * block + k, block, stride=2), :] = picked

    gate = gate_ref[...].astype(F32)
    hf[...] = gate * jax.nn.sigmoid(gate) * up_ref[...].astype(F32)
    for k in range(2):
        ht[0, k * cols:(k + 1) * cols, :] = hf[pl.ds(k, tokens, stride=2), :].T.astype(BF16)
    ht[0, 2 * cols:2 * cols + 16, :] = named_ref[...]

    pl.semaphore_wait(row_sem, len(column))
    for device in levels:
        greet(plane_sem, device)
    z_step(1)
    z_step(2)
    direct(0, 0)
    z_step(3)
    direct(1, 0)
    forward(0, 0)
    z_step(4)
    direct(2, 0)
    start(to_beside)
    start(hidden_copy)
    pl.semaphore_wait(plane_sem, len(levels))
    send_weights()
    turn(0)
    forward(1, 0)
    forward(2, 0)
    turn(1)
    turn(2)
    to_beside.wait_recv()
    start(relay)
    hidden_copy.wait_recv()
    lax.fori_loop(0, CELLS, send_beside, 0)
    forward(0, 1)
    forward(1, 1)
    arrived(0, 1)
    to_core.wait_recv()
    relay.wait_recv()
    backward(0)
    forward(2, 1)
    arrived(1, 1)
    backward(1)
    arrived(2, 1)
    backward(2)

    wide_piece = CELLS * rows
    targets = (toward, far, z_hi, away)

    def over_chip(s):
        return remote(gx.at[s], gy.at[s], xs.at[s], xr.at[s], other)

    def over_pair(slot):
        return remote(px.at[slot], py.at[slot], ps.at[slot], pr.at[slot], at_lo(beside))

    def gradient(s):
        begin = targets[s] * wide_piece

        def tile(t, carry):
            lane = pl.multiple_of(begin + t * 256, 256)
            gf[s, :, pl.ds(pl.multiple_of(t * 256, 256), 256)] = jnp.dot(
                htq[...], x2[:, pl.ds(lane, 256)], preferred_element_type=F32
            )
            return carry

        lax.fori_loop(0, wide_piece // 256, tile, 0)
        gx[s, 0] = gf[s, expert_lanes(side, 1 - core), :].astype(BF16)
        gx[s, 1] = gf[s, expert_lanes(1 - side, 1 - core), :].astype(BF16)
        start(over_chip(s))

    def chip_sum(s, own):
        lanes = expert_lanes(side, core) if own else expert_lanes(1 - side, core)
        return gf[s, lanes, :] + gy[s, 0 if own else 1].astype(F32)

    def sum_chip(s):
        over_chip(s).wait_recv()
        if s == 0:
            px[0] = chip_sum(0, True).astype(BF16)
            start(over_pair(0))
            px[1] = chip_sum(0, False).astype(BF16)
            start(over_pair(1))
        elif s == 1:
            px[2] = chip_sum(1, True).astype(BF16)
            start(over_pair(2))
            gu[0] = chip_sum(1, False)
        elif s == 2:
            px[3] = chip_sum(2, False).astype(BF16)
            start(over_pair(3))
            gu[1] = chip_sum(2, True)
        else:
            gu[2] = chip_sum(3, True)
            gu[3] = chip_sum(3, False)

    def deliver(part_sum, slot, lo, hi, near):
        over_pair(slot).wait_recv()
        total = gu[part_sum] + py[slot].astype(F32)
        gst[part_sum * wide_piece:(part_sum + 1) * wide_piece, :] = total.T.astype(BF16)

        def rows_of(c):
            return gst.at[pl.ds(pl.multiple_of(part_sum * wide_piece + c * rows, rows), rows), :]

        def send(i, carry):
            c = (cell + i) % CELLS
            remote(rows_of(c), gr_ref.at[:, my_lanes], gs.at[0], grs.at[0], owner(lo, hi, c)).start()
            return carry

        if near:
            pltpu.make_async_copy(rows_of(cell), gr_ref.at[:, my_lanes], grs.at[0]).start()
        lax.fori_loop(1 if near else 0, CELLS, send, 0)

    gradient(1)
    gradient(0)
    sum_chip(1)
    sum_chip(0)
    for q in range(SLOTS):
        dh_copy(q).start()
    gradient(2)
    gradient(3)
    deliver(0, 2, beside, far, False)
    sum_chip(2)
    sum_chip(3)
    deliver(3, 0, beside, away, False)
    deliver(2, 1, z_lo, away, False)
    deliver(1, 3, z_lo, z_hi, True)

    for copy in sends:
        copy.wait_send()
    for q in range(SLOTS):
        if (q - OWN) % 2 != 0:
            dh_copy(q).wait_send()
    sent = w_ref.at[pl.ds(0, (NHI * CELLS - 1) * rows), :]
    pltpu.make_async_copy(sent, sent, ws.at[0]).wait()
    sent = gst.at[pl.ds(0, (NHI * CELLS - 1) * rows), :]
    pltpu.make_async_copy(sent, sent, gs.at[0]).wait()
    pltpu.make_async_copy(wr_ref, wr_ref, wr.at[0]).wait()
    pltpu.make_async_copy(dr_ref, dr_ref, drecv.at[0]).wait()
    pltpu.make_async_copy(da_ref, da_ref, drecv.at[1]).wait()
    pltpu.make_async_copy(gr_ref, gr_ref, grs.at[0]).wait()


def exchange_all(og, weight, gate, up, named):
    half = og.shape[1]
    width, cols = weight.shape
    tokens = named.shape[1]
    rows = width // (NHI * CELLS)
    ff = cols * NHI * CELLS
    total = SLOTS * CELLS * 8
    piece = width // NHI
    any_space = pl.BlockSpec(memory_space=pl.ANY)
    vmem = pl.BlockSpec(memory_space=pltpu.VMEM)
    dma = pltpu.SemaphoreType.DMA
    ranges = len(RANGES)
    return pl.pallas_call(
        kernel,
        out_shape=(
            jax.ShapeDtypeStruct((rows, ff), BF16),
            jax.ShapeDtypeStruct((rows, ff), BF16),
            jax.ShapeDtypeStruct((2 * tokens, cols), F32),
            jax.ShapeDtypeStruct((2 * tokens, cols), F32),
        ),
        in_specs=[vmem] * 5,
        out_specs=(any_space,) * 4,
        scratch_shapes=[
            pltpu.VMEM((SLOTS, NX, NY, 16, half), BF16),
            pltpu.VMEM((total, width), BF16),
            pltpu.VMEM((width, PAIR * cols), BF16),
            pltpu.VMEM((2 * tokens, cols), F32),
            pltpu.VMEM((2, 2 * cols + 16, tokens), BF16),
            pltpu.VMEM((PAIR * cols, total), BF16),
            pltpu.VMEM((SLOTS, 2, PAIR, CELLS * 8, cols), F32),
            pltpu.VMEM((total, PAIR * cols), F32),
            pltpu.VMEM((2 * total, cols), F32),
            pltpu.VMEM((NHI, PAIR * cols, piece), F32),
            pltpu.VMEM((NHI, 2, cols, piece), BF16),
            pltpu.VMEM((NHI, 2, cols, piece), BF16),
            pltpu.VMEM((NHI, cols, piece), F32),
            pltpu.VMEM((NHI, cols, piece), BF16),
            pltpu.VMEM((NHI, cols, piece), BF16),
            pltpu.VMEM((width, cols), BF16),
            dma((SLOTS,)), dma((SLOTS,)),
            dma((ranges, 2, 2, 4)), dma((ranges, 2, 2, 4)),
            dma((1,)), dma((1,)),
            dma((1,)), dma((1,)),
            dma((SLOTS,)), dma((2,)),
            dma((NHI,)), dma((NHI,)),
            dma((NHI,)), dma((NHI,)),
            dma((1,)), dma((1,)),
            dma((3,)), dma((3,)),
            pltpu.SemaphoreType.REGULAR, pltpu.SemaphoreType.REGULAR,
        ],
        compiler_params=pltpu.CompilerParams(
            collective_id=0, has_side_effects=True, vmem_limit_bytes=56 * 1024 * 1024
        ),
    )(og, weight, gate, up, named)


def body(out_grad, gate_saved, up_saved, routing, down_weight, momentum):
    group_tok, topk, cols = gate_saved.shape
    own_tok, width = out_grad.shape
    half = width // 2
    og = out_grad.reshape(own_tok, 2, half).transpose(1, 0, 2).reshape(2 * own_tok, half)
    gate = gate_saved.astype(F32)
    up = up_saved.astype(F32)
    sigma = jax.nn.sigmoid(gate)
    named = jnp.pad(routing.T.astype(BF16), ((0, 16 - topk), (0, 0)))
    flat = (group_tok * topk, cols)
    shard_weight, shard_grad, near, across = exchange_all(
        og, down_weight[0], gate_saved.reshape(flat), up_saved.reshape(flat), named
    )
    dh = near.reshape(gate.shape) + across.reshape(gate.shape)
    d_up = (dh * gate * sigma).astype(BF16)
    d_gate = (dh * up * sigma * (1.0 + gate * (1.0 - sigma))).astype(BF16)

    grad = shard_grad[None].astype(F32)
    moment = momentum.astype(F32)
    mix = beta_first * moment + (1.0 - beta_first) * grad
    new_weight = shard_weight[None].astype(F32) * (
        1.0 - step_rate * decay_rate
    ) - step_rate * jnp.tanh(mix / sign_width)
    new_momentum = (beta_second * moment + (1.0 - beta_second) * grad).astype(BF16)
    return (d_gate, d_up, new_weight, new_momentum)


def solution(mesh):
    placed = (
        P(("expert", "dp"), None),
        P("expert", None, "dp"),
        P("expert", None, "dp"),
        P("expert", None),
        P("expert", None, "dp"),
        P("expert", "dp", None),
    )
    return jax.shard_map(
        body,
        mesh=mesh,
        in_specs=placed,
        out_specs=(
            P("expert", None, "dp"),
            P("expert", None, "dp"),
            P("expert", "dp", None),
            P("expert", "dp", None),
        ),
        check_vma=False,
    )
```

```python
import functools

import jax
import jax.numpy as jnp
from jax import lax
from jax.experimental import pallas as pl
from jax.experimental.pallas import tpu as pltpu
from jax.sharding import PartitionSpec as P

beta_first = 0.9
beta_second = 0.99
step_rate = 0.01
decay_rate = 1.0
sign_width = 10.0

NZ, NX, NY, NLO, NHI = 16, 4, 4, 4, 4
CELLS = NX * NY
PAIR = 4
SLOTS = NZ // 2
OWN = SLOTS // 2 - 1
RANGES = ((2, 4), (0, 2), (6, 2))
BF16, F32 = jnp.bfloat16, jnp.float32


def kernel(
    og_ref, w_ref, gate_ref, up_ref, named_ref, wr_ref, gr_ref, dr_ref, da_ref,
    xb, x2, wp, hf, ht, htq, mk, dn, ds, gf, gx, gy, gu, px, py, gst,
    zs, zr, ags, agr, ws, wr, hs, hr, dsend, drecv, xs, xr, ps, pr, gs, grs, was, war,
    row_sem, plane_sem,
):
    half = og_ref.shape[1]
    cols = w_ref.shape[1]
    expert, dp = lax.axis_index("expert"), lax.axis_index("dp")
    core, z_lo = expert % 2, expert // 2
    z_hi, x, y = dp // CELLS, (dp // NY) % NX, dp % NY
    cell = dp % CELLS
    z = z_hi * NLO + z_lo
    side, pair = z_lo % 2, z_lo // 2
    beside = pair * 2 + 1 - side
    across = (z_lo + 2) % NLO

    def at_z(zz):
        return {"expert": (zz % NLO) * 2 + core, "dp": (zz // NLO) * CELLS + cell}

    def at_cell(xx, yy):
        return {"expert": expert, "dp": z_hi * CELLS + xx * NY + yy}

    def at_lo(lo):
        return {"expert": lo * 2 + core, "dp": dp}

    away = (z_hi + NHI - 1 + 2 * side) % NHI
    toward = (z_hi + 1 + 2 * side) % NHI
    far = (z_hi + 2) % NHI

    def owner(lo, hi, c):
        return {"expert": lo * 2 + core, "dp": hi * CELLS + c}

    z_up, z_down = at_z((z + 2) % NZ), at_z((z + NZ - 2) % NZ)
    other = {"expert": z_lo * 2 + 1 - core, "dp": dp}

    def remote(src, dst, send, recv, device):
        return pltpu.make_async_remote_copy(
            src_ref=src, dst_ref=dst, send_sem=send, recv_sem=recv,
            device_id=device, device_id_type=pl.DeviceIdType.MESH,
        )

    barrier = pltpu.get_barrier_semaphore()

    def greet(semaphore, device):
        pl.semaphore_signal(
            semaphore, inc=1, device_id=device, device_id_type=pl.DeviceIdType.MESH
        )

    column = [at_cell(x, (y + i) % NY) for i in range(1, NY)]
    levels = [owner(z_lo, (z_hi + i) % NHI, cell) for i in range(1, NHI)]
    levels += [owner(beside, (z_hi + i) % NHI, cell) for i in range(NHI)]
    nearby = [z_up, z_down, other, at_lo(across)]
    nearby += [at_cell((x + i) % NX, y) for i in range(1, NX)] + column + levels
    for device in nearby:
        greet(barrier, device)

    def expert_lanes(s, c):
        return pl.ds(pl.multiple_of((s * 2 + c) * cols, cols), cols)

    xb[OWN, x, y] = og_ref[...]
    wp[:, expert_lanes(side, core)] = w_ref[...]
    pl.semaphore_wait(barrier, len(nearby))

    def z_copy(q, step):
        device = z_down if step > 0 else z_up
        return remote(xb.at[q, x, y], xb.at[q + step, x, y], zs.at[q + step], zr.at[q + step], device)

    sends = []

    def start(copy):
        copy.start()
        sends.append(copy)

    def z_step(k):
        z_copy(OWN + k - 1, 1).wait_recv()
        if OWN + k < SLOTS - 1:
            start(z_copy(OWN + k, 1))
        if OWN - k >= 0:
            z_copy(OWN - k + 1, -1).wait_recv()
            if OWN - k > 0:
                start(z_copy(OWN - k, -1))

    start(z_copy(OWN, 1))
    start(z_copy(OWN, -1))

    own_weight = wp.at[:, expert_lanes(side, core)]
    to_core = remote(w_ref, own_weight, was.at[0], war.at[0], other)
    to_beside = remote(w_ref, own_weight, was.at[1], war.at[1], at_lo(beside))
    from_beside = wp.at[:, expert_lanes(1 - side, core)]
    relay = remote(from_beside, from_beside, was.at[2], war.at[2], other)
    start(to_core)
    for device in column:
        greet(row_sem, device)

    hidden_copy = remote(ht.at[0], ht.at[1], hs.at[0], hr.at[0], at_lo(across))

    part = half // 2
    piece = part // 2

    def place(r, path, phase, source, first, width):
        slots = pl.ds(RANGES[r][0], RANGES[r][1])
        lanes = pl.ds(path * part + first, width)
        if phase == 0:
            return xb.at[slots, source, y, :, lanes] if path == 0 else xb.at[slots, x, source, :, lanes]
        return xb.at[slots, :, source, :, lanes] if path == 0 else xb.at[slots, source, :, :, lanes]

    def cell_copy(r, path, phase, kind):
        along_x = path == phase
        size = NX if along_x else NY
        mine = x if along_x else y
        right, left = (mine + 1) % size, (mine + size - 1) % size
        to = right if kind in (0, 2) else left
        device = at_cell(to, y) if along_x else at_cell(x, to)
        source = (mine, mine, left, right)[kind]
        first, width = ((0, part), (0, part), (0, piece), (piece, piece))[kind]
        ref = place(r, path, phase, source, first, width)
        return remote(ref, ref, ags.at[r, path, phase, kind], agr.at[r, path, phase, kind], device)

    def direct(r, phase):
        for path in range(2):
            start(cell_copy(r, path, phase, 0))
            start(cell_copy(r, path, phase, 1))

    def forward(r, phase):
        for path in range(2):
            for kind in (0, 1):
                cell_copy(r, path, phase, kind).wait_recv()
                start(cell_copy(r, path, phase, kind + 2))

    def arrived(r, phase):
        for path in range(2):
            for kind in (2, 3):
                cell_copy(r, path, phase, kind).wait_recv()

    def turn(r):
        arrived(r, 0)
        direct(r, 1)

    rows = wr_ref.shape[0]
    my_lanes = pl.ds(pl.multiple_of(dp * cols, cols), cols)

    def weight_rows(s, hi, c):
        row = pl.multiple_of((hi * CELLS + c) * rows, rows)
        return wp.at[pl.ds(row, rows), expert_lanes(s, core)]

    def send_weight(lo, s, hi, c):
        remote(weight_rows(s, hi, c), wr_ref.at[:, my_lanes], ws.at[0], wr.at[0], owner(lo, hi, c)).start()

    def send_own(i, carry):
        send_weight(z_lo, side, away, (cell + i) % CELLS)
        return carry

    def send_near(i, carry):
        send_weight(z_lo, side, z_hi, (cell + i) % CELLS)
        return carry

    def send_beside(i, carry):
        send_weight(beside, 1 - side, far, (cell + i) % CELLS)
        send_weight(beside, 1 - side, away, (cell + i) % CELLS)
        return carry

    def send_weights():
        pltpu.make_async_copy(weight_rows(side, z_hi, cell), wr_ref.at[:, my_lanes], wr.at[0]).start()
        lax.fori_loop(0, CELLS, send_own, 0)
        lax.fori_loop(1, CELLS, send_near, 0)

    block = CELLS * 8
    tokens = named_ref.shape[1]

    def token_lane(q):
        return pl.multiple_of(((z + 2 * (q + SLOTS - OWN)) % NZ) // NLO * block, block)

    def unpack_hidden(q):
        lane = token_lane(q)
        which = (q - OWN) % 2
        named = ht[which, 2 * cols:2 * cols + 16, pl.ds(lane, block)].astype(F32)
        first = ht[which, 0:cols, pl.ds(lane, block)].astype(F32)
        second = ht[which, cols:2 * cols, pl.ds(lane, block)].astype(F32)
        hits = []
        for e in range(PAIR):
            index = (pair * PAIR + e).astype(F32)
            one = jnp.where(named[0:1] == index, 1.0, 0.0)
            two = jnp.where(named[1:2] == index, 1.0, 0.0)
            hits.append((one, two))
            htq[e * cols:(e + 1) * cols, q * block:(q + 1) * block] = (one * first + two * second).astype(BF16)
        for k in range(2):
            for e in range(PAIR):
                mk[q, k, e] = jnp.broadcast_to(hits[e][k], (block, block)).T

    def unpack(q, carry):
        row = pl.multiple_of(q * block, block)
        for first in range(0, half, 256):
            wide = xb[q, :, :, :, first:first + 256].astype(F32).reshape(CELLS, 16, 256)
            x2[pl.ds(row, block), first:first + 256] = wide[:, 0:8].reshape(block, 256).astype(BF16)
            x2[pl.ds(row, block), half + first:half + first + 256] = (
                wide[:, 8:16].reshape(block, 256).astype(BF16)
            )
        return carry

    def dh_copy(q):
        src = ds.at[pl.ds(q * 2 * block, 2 * block), :]
        row = pl.multiple_of(2 * token_lane(q), 2 * block)
        if (q - OWN) % 2 == 0:
            return pltpu.make_async_copy(src, dr_ref.at[pl.ds(row, 2 * block), :], drecv.at[0])
        return remote(src, da_ref.at[pl.ds(row, 2 * block), :], dsend.at[q], drecv.at[1], at_lo(across))

    def backward(r):
        first, slots = RANGES[r]
        lax.fori_loop(first, first + slots, unpack, 0)
        low, high = first * block, (first + slots) * block
        dn[low:high, :] = jnp.dot(x2[low:high, :], wp[...], preferred_element_type=F32)
        for q in range(first, first + slots):
            unpack_hidden(q)
            at = slice(q * block, (q + 1) * block)
            for k in range(2):
                picked = mk[q, k, 0] * dn[at, 0:cols]
                for e in range(1, PAIR):
                    picked += mk[q, k, e] * dn[at, e * cols:(e + 1) * cols]
                ds[pl.ds(q * 2 * block + k, block, stride=2), :] = picked

    gate = gate_ref[...].astype(F32)
    hf[...] = gate * jax.nn.sigmoid(gate) * up_ref[...].astype(F32)
    for k in range(2):
        ht[0, k * cols:(k + 1) * cols, :] = hf[pl.ds(k, tokens, stride=2), :].T.astype(BF16)
    ht[0, 2 * cols:2 * cols + 16, :] = named_ref[...]

    pl.semaphore_wait(row_sem, len(column))
    for device in levels:
        greet(plane_sem, device)
    z_step(1)
    z_step(2)
    direct(0, 0)
    z_step(3)
    start(to_beside)
    start(hidden_copy)
    direct(1, 0)
    forward(0, 0)
    z_step(4)
    direct(2, 0)
    pl.semaphore_wait(plane_sem, len(levels))
    send_weights()
    turn(0)
    forward(1, 0)
    forward(2, 0)
    turn(1)
    turn(2)
    to_beside.wait_recv()
    start(relay)
    hidden_copy.wait_recv()
    lax.fori_loop(0, CELLS, send_beside, 0)
    forward(0, 1)
    forward(1, 1)
    arrived(0, 1)
    to_core.wait_recv()
    relay.wait_recv()
    backward(0)
    forward(2, 1)
    arrived(1, 1)
    backward(1)
    arrived(2, 1)
    backward(2)

    wide_piece = CELLS * rows
    targets = (toward, far, z_hi, away)

    def over_chip(s):
        return remote(gx.at[s], gy.at[s], xs.at[s], xr.at[s], other)

    def over_pair(slot):
        return remote(px.at[slot], py.at[slot], ps.at[slot], pr.at[slot], at_lo(beside))

    def gradient(s):
        begin = targets[s] * wide_piece

        def tile(t, carry):
            lane = pl.multiple_of(begin + t * 256, 256)
            gf[s, :, pl.ds(pl.multiple_of(t * 256, 256), 256)] = jnp.dot(
                htq[...], x2[:, pl.ds(lane, 256)], preferred_element_type=F32
            )
            return carry

        lax.fori_loop(0, wide_piece // 256, tile, 0)
        gx[s, 0] = gf[s, expert_lanes(side, 1 - core), :].astype(BF16)
        gx[s, 1] = gf[s, expert_lanes(1 - side, 1 - core), :].astype(BF16)
        start(over_chip(s))

    def chip_sum(s, own):
        lanes = expert_lanes(side, core) if own else expert_lanes(1 - side, core)
        return gf[s, lanes, :] + gy[s, 0 if own else 1].astype(F32)

    def sum_chip(s):
        over_chip(s).wait_recv()
        if s == 0:
            px[0] = chip_sum(0, True).astype(BF16)
            start(over_pair(0))
            px[1] = chip_sum(0, False).astype(BF16)
            start(over_pair(1))
        elif s == 1:
            px[2] = chip_sum(1, True).astype(BF16)
            start(over_pair(2))
            gu[0] = chip_sum(1, False)
        elif s == 2:
            px[3] = chip_sum(2, False).astype(BF16)
            start(over_pair(3))
            gu[1] = chip_sum(2, True)
        else:
            gu[2] = chip_sum(3, True)
            gu[3] = chip_sum(3, False)

    def deliver(part_sum, slot, lo, hi, near):
        over_pair(slot).wait_recv()
        total = gu[part_sum] + py[slot].astype(F32)
        gst[part_sum * wide_piece:(part_sum + 1) * wide_piece, :] = total.T.astype(BF16)

        def rows_of(c):
            return gst.at[pl.ds(pl.multiple_of(part_sum * wide_piece + c * rows, rows), rows), :]

        def send(i, carry):
            c = (cell + i) % CELLS
            remote(rows_of(c), gr_ref.at[:, my_lanes], gs.at[0], grs.at[0], owner(lo, hi, c)).start()
            return carry

        if near:
            pltpu.make_async_copy(rows_of(cell), gr_ref.at[:, my_lanes], grs.at[0]).start()
        lax.fori_loop(1 if near else 0, CELLS, send, 0)

    gradient(1)
    gradient(0)
    sum_chip(1)
    sum_chip(0)
    for q in range(SLOTS):
        dh_copy(q).start()
    gradient(2)
    gradient(3)
    deliver(0, 2, beside, far, False)
    sum_chip(2)
    sum_chip(3)
    deliver(3, 0, beside, away, False)
    deliver(2, 1, z_lo, away, False)
    deliver(1, 3, z_lo, z_hi, True)

    for copy in sends:
        copy.wait_send()
    for q in range(SLOTS):
        if (q - OWN) % 2 != 0:
            dh_copy(q).wait_send()
    sent = w_ref.at[pl.ds(0, (NHI * CELLS - 1) * rows), :]
    pltpu.make_async_copy(sent, sent, ws.at[0]).wait()
    sent = gst.at[pl.ds(0, (NHI * CELLS - 1) * rows), :]
    pltpu.make_async_copy(sent, sent, gs.at[0]).wait()
    pltpu.make_async_copy(wr_ref, wr_ref, wr.at[0]).wait()
    pltpu.make_async_copy(dr_ref, dr_ref, drecv.at[0]).wait()
    pltpu.make_async_copy(da_ref, da_ref, drecv.at[1]).wait()
    pltpu.make_async_copy(gr_ref, gr_ref, grs.at[0]).wait()


def exchange_all(og, weight, gate, up, named):
    half = og.shape[1]
    width, cols = weight.shape
    tokens = named.shape[1]
    rows = width // (NHI * CELLS)
    ff = cols * NHI * CELLS
    total = SLOTS * CELLS * 8
    piece = width // NHI
    any_space = pl.BlockSpec(memory_space=pl.ANY)
    vmem = pl.BlockSpec(memory_space=pltpu.VMEM)
    dma = pltpu.SemaphoreType.DMA
    ranges = len(RANGES)
    return pl.pallas_call(
        kernel,
        out_shape=(
            jax.ShapeDtypeStruct((rows, ff), BF16),
            jax.ShapeDtypeStruct((rows, ff), BF16),
            jax.ShapeDtypeStruct((2 * tokens, cols), F32),
            jax.ShapeDtypeStruct((2 * tokens, cols), F32),
        ),
        in_specs=[vmem] * 5,
        out_specs=(any_space,) * 4,
        scratch_shapes=[
            pltpu.VMEM((SLOTS, NX, NY, 16, half), BF16),
            pltpu.VMEM((total, width), BF16),
            pltpu.VMEM((width, PAIR * cols), BF16),
            pltpu.VMEM((2 * tokens, cols), F32),
            pltpu.VMEM((2, 2 * cols + 16, tokens), BF16),
            pltpu.VMEM((PAIR * cols, total), BF16),
            pltpu.VMEM((SLOTS, 2, PAIR, CELLS * 8, cols), F32),
            pltpu.VMEM((total, PAIR * cols), F32),
            pltpu.VMEM((2 * total, cols), F32),
            pltpu.VMEM((NHI, PAIR * cols, piece), F32),
            pltpu.VMEM((NHI, 2, cols, piece), BF16),
            pltpu.VMEM((NHI, 2, cols, piece), BF16),
            pltpu.VMEM((NHI, cols, piece), F32),
            pltpu.VMEM((NHI, cols, piece), BF16),
            pltpu.VMEM((NHI, cols, piece), BF16),
            pltpu.VMEM((width, cols), BF16),
            dma((SLOTS,)), dma((SLOTS,)),
            dma((ranges, 2, 2, 4)), dma((ranges, 2, 2, 4)),
            dma((1,)), dma((1,)),
            dma((1,)), dma((1,)),
            dma((SLOTS,)), dma((2,)),
            dma((NHI,)), dma((NHI,)),
            dma((NHI,)), dma((NHI,)),
            dma((1,)), dma((1,)),
            dma((3,)), dma((3,)),
            pltpu.SemaphoreType.REGULAR, pltpu.SemaphoreType.REGULAR,
        ],
        compiler_params=pltpu.CompilerParams(
            collective_id=0, has_side_effects=True, vmem_limit_bytes=56 * 1024 * 1024
        ),
    )(og, weight, gate, up, named)


def body(out_grad, gate_saved, up_saved, routing, down_weight, momentum):
    group_tok, topk, cols = gate_saved.shape
    own_tok, width = out_grad.shape
    half = width // 2
    og = out_grad.reshape(own_tok, 2, half).transpose(1, 0, 2).reshape(2 * own_tok, half)
    gate = gate_saved.astype(F32)
    up = up_saved.astype(F32)
    sigma = jax.nn.sigmoid(gate)
    named = jnp.pad(routing.T.astype(BF16), ((0, 16 - topk), (0, 0)))
    flat = (group_tok * topk, cols)
    shard_weight, shard_grad, near, across = exchange_all(
        og, down_weight[0], gate_saved.reshape(flat), up_saved.reshape(flat), named
    )
    dh = near.reshape(gate.shape) + across.reshape(gate.shape)
    d_up = (dh * gate * sigma).astype(BF16)
    d_gate = (dh * up * sigma * (1.0 + gate * (1.0 - sigma))).astype(BF16)

    grad = shard_grad[None].astype(F32)
    moment = momentum.astype(F32)
    mix = beta_first * moment + (1.0 - beta_first) * grad
    new_weight = shard_weight[None].astype(F32) * (
        1.0 - step_rate * decay_rate
    ) - step_rate * jnp.tanh(mix / sign_width)
    new_momentum = (beta_second * moment + (1.0 - beta_second) * grad).astype(BF16)
    return (d_gate, d_up, new_weight, new_momentum)


def solution(mesh):
    placed = (
        P(("expert", "dp"), None),
        P("expert", None, "dp"),
        P("expert", None, "dp"),
        P("expert", None),
        P("expert", None, "dp"),
        P("expert", "dp", None),
    )
    return jax.shard_map(
        body,
        mesh=mesh,
        in_specs=placed,
        out_specs=(
            P("expert", None, "dp"),
            P("expert", None, "dp"),
            P("expert", "dp", None),
            P("expert", "dp", None),
        ),
        check_vma=False,
    )
```
